512 devices in a mesh: seq: 16 (over y, z_hi), own: 32 (over z_lo, x, core).
Axes of the slice: x: 4, y: 4, z: 16 (z_hi: 4, z_lo: 4; z = z_hi * 4 + z_lo), core: 2. Of those that a mesh axis runs over, the one named last changes fastest.
Arguments:
- queries: bfloat16 [32, 2048, 1024], P('own', 'seq'), may hold values from -6 to 6
- keys: bfloat16 [32, 2048, 1024], P('own', 'seq'), may hold values from -6 to 6
- values: bfloat16 [32, 2048, 1024], P('own', 'seq'), may hold values from -6 to 6
- gates: bfloat16 [32, 2048, 1024], P('own', 'seq'), may hold values from -6 to 6
- lengths: int32 [32, 4], P('own'), may hold values from 1 to 1024, 2048 in all within a row
- gain: float32 [1024], replicated, may hold values from 0.1 to 1.9
- grad_out: bfloat16 [32, 2048, 1024], P('own', 'seq'), may hold values from -6 to 6
Outputs:
- output: bfloat16 [32, 2048, 1024], P('own', 'seq')
- grad_queries: bfloat16 [32, 2048, 1024], P('own', 'seq')
- grad_keys: bfloat16 [32, 2048, 1024], P('own', 'seq')
- grad_values: bfloat16 [32, 2048, 1024], P('own', 'seq')
- grad_gates: bfloat16 [32, 2048, 1024], P('own', 'seq')
- grad_gain: float32 [1024], replicated
The draws below stay inside these ranges and needn't reach their ends.
Inputs may be any that keep to these rules, and one draw needn't show every extreme that they name: Each group's 4 lengths sum to 2048; in every group the longest is exactly 1024.
All inputs are finite; a program needn't handle non-finite values.
Results may differ from the reference program's by a relative error of at most 0.0058.
Values may be sent and summed in bfloat16 or wider, within the bound.
No kernel may reach another device: no remote copies, remote signals or barrier semaphores. Data moves between devices by JAX's collectives and lax.ppermute only.
A program may use at most 128 MiB of HBM per device.

```python
import math
import jax
import jax.numpy as jnp
import numpy as np
from jax import lax

D = 1024
H = 8
USERS = 4
SEQLEN = 2048
MAXLEN = 1024
GROUPS = 32


def level_of(own_key, dims, shards, low, largest):
    def one(dim, parts):
        draws = jax.random.uniform(jax.random.fold_in(jax.random.fold_in(own_key, 6), dim), (parts,), jnp.float32, low / len(shards), largest / len(shards))
        return jnp.repeat(jnp.exp(draws), dims[dim] // parts).reshape((-1,) + (1,) * (len(dims) - dim - 1))

    level = one(*shards[0])
    for cut in shards[1:]:
        level = level * one(*cut)
    return level


def length_profile(count, total, bound, lean):
    loads = [(1 << 20) // math.isqrt(rank ** lean) + 1 for rank in range(2, count + 1)]
    spare, counts = total - bound - (count - 1), [1] * (count - 1)
    while spare > 0:
        candidates = [i for i in range(count - 1) if counts[i] < bound]
        whole, left = sum([loads[i] for i in candidates]), spare
        for i in candidates:
            more = min(bound - counts[i], max(1, left * loads[i] // whole), spare)
            counts[i] = counts[i] + more
            spare = spare - more
    return np.array([bound] + counts)


def uneven_parts(key, number_of, total, most, lean):
    if number_of == 2:
        one = jax.random.randint(key, (), max(1, total - most), min(most, total - 1) + 1)
        return jnp.stack([one, total - one])
    sizes = jnp.asarray(length_profile(number_of, total, most, lean), jnp.int32)
    twos = (number_of - 1) // 2
    source_of, taker = sizes[1:1 + 2 * twos:2], sizes[2:2 + 2 * twos:2]
    slack = jnp.minimum(source_of - 1, most - taker)
    moved = jax.random.randint(jax.random.fold_in(key, 1), (twos,), 0, 1 << 20) % (slack + 1)
    sizes = sizes.at[1:1 + 2 * twos:2].set(source_of - moved).at[2:2 + 2 * twos:2].set(taker + moved)
    return sizes[jax.random.permutation(jax.random.fold_in(key, 2), number_of)]


def noise(key, extent, scale, limit, shards=(), kind=jnp.bfloat16):
    entries = jax.random.normal(key, extent, jnp.float32) * scale
    if len(shards) > 0:
        entries = level_of(key, extent, shards, -0.22, 0.18) * entries
    return jnp.clip(entries, min=-limit, max=limit).astype(kind)


def setup_inputs(seed: int = 0) -> dict:
    streams_of = jax.random.split(jax.random.key(seed), 8)
    queries = noise(streams_of[0], (GROUPS, SEQLEN, D), 1.0, 6.0, ((0, 32), (1, 16)))
    keys = noise(streams_of[1], (GROUPS, SEQLEN, D), 1.0, 6.0, ((0, 32), (1, 16)))
    values = noise(streams_of[2], (GROUPS, SEQLEN, D), 1.0, 6.0, ((0, 32), (1, 16)))
    gates = noise(streams_of[3], (GROUPS, SEQLEN, D), 1.0, 6.0, ((0, 32), (1, 16)))
    lengths = jax.vmap(lambda own: uneven_parts(own, USERS, SEQLEN, MAXLEN, 2))(jax.random.split(streams_of[4], GROUPS)).reshape((GROUPS, USERS)).astype(jnp.int32)
    gain = jnp.clip(1.0 + 0.18 * jax.random.normal(streams_of[5], (D,), jnp.float32), 0.1, 1.9)
    grad_out = noise(streams_of[6], (GROUPS, SEQLEN, D), 1.0, 6.0, ((0, 32), (1, 16)))
    return {"queries": queries, "keys": keys, "values": values, "gates": gates, "lengths": lengths, "gain": gain, "grad_out": grad_out}


def positions_info(pos, lens):
    ends = jnp.cumsum(lens)
    seg = lax.optimization_barrier(jnp.sum((pos[:, None] >= ends[None, :]).astype(jnp.int32), axis=1))
    users = jnp.arange(lens.shape[0], dtype=jnp.int32)
    span = lax.optimization_barrier(jnp.sum(jnp.where(seg[:, None] == users[None, :], lens[None, :], 0), axis=1))
    return (seg, 1.0 / span.astype(jnp.float32))

def silu_slope(scores):
    sig = jax.nn.sigmoid(scores)
    return sig * (1.0 + scores * (1.0 - sig))

def reference(queries, keys, values, gates, lengths, gain, grad_out):

    def one_group(item):
        query, key, value, gate, lens, grad = item
        seq_len, width = query.shape
        head_size = width // H
        scale = 1.0 / math.sqrt(head_size)
        pos = jnp.arange(seq_len, dtype=jnp.int32)
        seg, inverse = positions_info(pos, lens)
        allowed = (seg[:, None] == seg[None, :]) & (pos[None, :] <= pos[:, None])
        weight = jnp.where(allowed, inverse[:, None], jnp.float32(0.0))
        q3 = query.astype(jnp.float32).reshape(seq_len, H, head_size)
        k3 = key.astype(jnp.float32).reshape(seq_len, H, head_size)
        v3 = value.astype(jnp.float32).reshape(seq_len, H, head_size)
        scores = jnp.einsum('thd,shd->hts', q3, k3) * scale
        probs = (jax.nn.silu(scores) * weight[None]).astype(jnp.bfloat16)
        attended = jnp.einsum('hts,shd->thd', probs.astype(jnp.float32), v3).reshape(seq_len, width)
        center = attended - lax.optimization_barrier(jnp.mean(attended, axis=1, keepdims=True))
        rstd = lax.rsqrt(lax.optimization_barrier(jnp.mean(center * center, axis=1, keepdims=True)) + 1e-05)
        normed = center * rstd
        gate_f = gate.astype(jnp.float32)
        grad_f = grad.astype(jnp.float32)
        output = (normed * gain[None, :] * gate_f).astype(jnp.bfloat16)
        grad_gate = (grad_f * normed * gain[None, :]).astype(jnp.bfloat16)
        gain_part = lax.optimization_barrier(jnp.sum(grad_f * gate_f * normed, axis=0))
        dnorm = grad_f * gate_f * gain[None, :]
        grad_att = rstd * (dnorm - lax.optimization_barrier(jnp.mean(dnorm, axis=1, keepdims=True)) - normed * lax.optimization_barrier(jnp.mean(dnorm * normed, axis=1, keepdims=True)))
        grad_att = grad_att.astype(jnp.bfloat16)
        ga3 = grad_att.astype(jnp.float32).reshape(seq_len, H, head_size)
        grad_probs = jnp.einsum('thd,shd->hts', ga3, v3)
        grad_scores = (grad_probs * weight[None] * silu_slope(scores)).astype(jnp.bfloat16)
        gs = grad_scores.astype(jnp.float32)
        grad_q = (jnp.einsum('hts,shd->thd', gs, k3) * scale).reshape(seq_len, width).astype(jnp.bfloat16)
        grad_k = (jnp.einsum('hts,thd->shd', gs, q3) * scale).reshape(seq_len, width).astype(jnp.bfloat16)
        grad_v = jnp.einsum('hts,thd->shd', probs.astype(jnp.float32), ga3).reshape(seq_len, width).astype(jnp.bfloat16)
        return (output, grad_q, grad_k, grad_v, grad_gate, gain_part)
    results = lax.map(one_group, (queries, keys, values, gates, lengths, grad_out))
    grad_gain = lax.optimization_barrier(jnp.sum(results[5], axis=0))
    return (results[0], results[1], results[2], results[3], results[4], grad_gain)
```

```python
import math

import jax
import jax.numpy as jnp
from jax import lax
from jax.experimental import pallas as pl
from jax.experimental.pallas import tpu as pltpu
from jax.sharding import PartitionSpec as P


H = 8
HALF = 64
HEAD = 128
TILE = 4
EXTRA = 16
F32 = jnp.float32
BF16 = jnp.bfloat16
VMEM_LIMIT = 48 * 1024 * 1024


def head_half(device):
    y, z = divmod(device, 4)
    return 2 * z + y // 2, y % 2


def dot(a, b, dims):
    return lax.dot_general(a, b, (dims, ((), ())), preferred_element_type=F32)


def iota(shape, dim):
    return lax.broadcasted_iota(jnp.int32, shape, dim)


def offsets(shape, dim):
    index = iota(shape, dim)
    return (index // HALF) * (2 * HALF) + index % HALF


def bounds(pos, info):
    start = jnp.zeros_like(pos)
    end = jnp.full_like(pos, 1 << 30)
    for user in range(info.shape[0] - 1):
        edge = info[1 + user]
        start = jnp.where(pos >= edge, jnp.maximum(start, edge), start)
        end = jnp.where(pos < edge, jnp.minimum(end, edge), end)
    return start, end - start


def tile_rows(ref, tile, first, last):
    block = ref[pl.ds(tile * TILE, TILE), first:last, :]
    return block.reshape(TILE * HALF, HEAD)


def first_key_tile(tile, info):
    start, _ = bounds(tile * (TILE * 2 * HALF) + info[0] * HALF, info)
    return start // (TILE * 2 * HALF)


def spread(column):
    square = iota((HALF, HEAD), 0) == iota((HALF, HEAD), 1)
    return jnp.sum(jnp.where(square, column, 0.0), axis=0, keepdims=True)


def gather_column(row):
    square = iota((HALF, HEAD), 0) == iota((HALF, HEAD), 1)
    return jnp.sum(jnp.where(square, row, 0.0), axis=1, keepdims=True)


def in_three(row):
    high = row.astype(BF16).astype(F32)
    mid = (row - high).astype(BF16).astype(F32)
    low = row - high - mid
    index = iota((EXTRA, HEAD), 0)
    block = jnp.where(index == 0, high, jnp.where(index == 1, mid, jnp.where(index == 2, low, 0.0)))
    return block.astype(BF16)


def pack_kernel(q_ref, k_ref, v_ref, out_ref):
    for device in range(out_ref.shape[0]):
        head, half = head_half(device)
        for part, ref in enumerate((q_ref, k_ref, v_ref)):
            out_ref[device, part * HALF : (part + 1) * HALF, :] = ref[
                half * HALF : (half + 1) * HALF, head * HEAD : (head + 1) * HEAD
            ]


def forward_tile(info, q_ref, kv_ref, kv_first, kv_half, tile, total):
    scale = 0.5 / math.sqrt(HEAD)
    span = TILE * 2 * HALF
    rows = TILE * HALF
    q = tile_rows(q_ref, tile, 0, HALF)
    pos = tile * span + info[0] * HALF + offsets((rows, 1), 0)
    start, _ = bounds(pos, info)
    where = offsets((1, rows), 1)

    def step(key_tile, total):
        k = tile_rows(kv_ref, key_tile, kv_first, kv_first + HALF)
        v = tile_rows(kv_ref, key_tile, kv_first + HALF, kv_first + 2 * HALF)
        base = key_tile * span + kv_half * HALF
        half_score = dot(q, k, ((1,), (1,))) * scale
        silu = half_score + half_score * jnp.tanh(half_score)
        allowed = (where >= start - base) & (where <= pos - base)
        probs = jnp.where(allowed, silu, 0.0).astype(BF16)
        return total + dot(probs, v, ((1,), (0,)))

    return lax.fori_loop(first_key_tile(tile, info), tile + 1, step, total)


def forward_own_kernel(info, mine_ref, sum_ref):
    rows = TILE * HALF
    for tile in range(mine_ref.shape[0] // TILE):
        total = jnp.zeros((rows, HEAD), F32)
        total = forward_tile(info, mine_ref, mine_ref, HALF, info[0], tile, total)
        sum_ref[tile * rows : (tile + 1) * rows, :] = total


def forward_other_kernel(info, mine_ref, other_ref, sum_ref, out_ref):
    rows = TILE * HALF
    for tile in range(mine_ref.shape[0] // TILE):
        total = sum_ref[tile * rows : (tile + 1) * rows, :]
        total = forward_tile(info, mine_ref, other_ref, 0, 1 - info[0], tile, total)
        pos = tile * TILE * 2 * HALF + info[0] * HALF + offsets((rows, 1), 0)
        _, length = bounds(pos, info)
        attended = total * (1.0 / length.astype(F32))
        mean = jnp.mean(attended, axis=1, keepdims=True).astype(BF16).astype(F32)
        rest = (attended - mean).astype(BF16)
        for part in range(TILE):
            span = slice(part * HALF, (part + 1) * HALF)
            slot = tile * TILE + part
            out_ref[slot, 0:HALF, :] = rest[span]
            out_ref[slot, HALF : HALF + EXTRA, :] = jnp.broadcast_to(
                spread(mean[span]), (EXTRA, HEAD)
            ).astype(BF16)


def norm_kernel(info, att_ref, gates_ref, grad_ref, gain_ref, out_ref, gate_grad_ref, att_grad_ref):
    width = H * HEAD
    devices = {head_half(device): device for device in range(att_ref.shape[0])}
    gain_sums = [jnp.zeros((1, HEAD), F32) for _ in range(H)]
    for half in range(2):
        span = slice(half * HALF, (half + 1) * HALF)
        attended = []
        for head in range(H):
            device = devices[head, half]
            mean = gather_column(att_ref[device, HALF : HALF + 1, :].astype(F32))
            attended.append(att_ref[device, 0:HALF, :].astype(F32) + mean)
        mean = jnp.sum(sum(attended), axis=1, keepdims=True) / width
        center = [block - mean for block in attended]
        var = jnp.sum(sum(block * block for block in center), axis=1, keepdims=True) / width
        rstd = lax.rsqrt(var + 1e-05)
        normed = [block * rstd for block in center]
        dnorm = []
        for head in range(H):
            cols = slice(head * HEAD, (head + 1) * HEAD)
            gain = gain_ref[0:1, cols]
            gate = gates_ref[span, cols].astype(F32)
            grad = grad_ref[span, cols].astype(F32)
            out_ref[span, cols] = (normed[head] * gain * gate).astype(BF16)
            gate_grad_ref[span, cols] = (grad * normed[head] * gain).astype(BF16)
            both = grad * gate
            gain_sums[head] = gain_sums[head] + jnp.sum(both * normed[head], axis=0, keepdims=True)
            dnorm.append(both * gain)
        first = jnp.sum(sum(dnorm), axis=1, keepdims=True) / width
        second = jnp.sum(sum(d * n for d, n in zip(dnorm, normed)), axis=1, keepdims=True) / width
        pos = info[info.shape[0] - 1] + half * HALF + iota((HALF, 1), 0)
        _, length = bounds(pos, info.at[0 : info.shape[0] - 1])
        factor = rstd * (1.0 / length.astype(F32))
        for head in range(H):
            grad_att = factor * (dnorm[head] - first - normed[head] * second)
            att_grad_ref[devices[head, half], 0:HALF, :] = grad_att.astype(BF16)
    for device in range(att_ref.shape[0]):
        att_grad_ref[device, HALF : HALF + EXTRA, :] = in_three(gain_sums[device // 2])


def backward_tiles(info, mine_ref, kv_ref, kv_first, kv_half, grad_ref, dq_ref, dk_ref, dv_ref):
    scale = 0.5 / math.sqrt(HEAD)
    span = TILE * 2 * HALF
    rows = TILE * HALF
    dk_ref[...] = jnp.zeros_like(dk_ref)
    dv_ref[...] = jnp.zeros_like(dv_ref)
    where = offsets((rows, 1), 0)
    for tile in range(mine_ref.shape[0] // TILE):
        q = tile_rows(mine_ref, tile, 0, HALF)
        grad = tile_rows(grad_ref, tile, 0, HALF)
        pos = tile * span + info[0] * HALF + offsets((1, rows), 1)
        start, _ = bounds(pos, info)

        def step(key_tile, total):
            k = tile_rows(kv_ref, key_tile, kv_first, kv_first + HALF)
            v = tile_rows(kv_ref, key_tile, kv_first + HALF, kv_first + 2 * HALF)
            base = key_tile * span + kv_half * HALF
            half_score = dot(k, q, ((1,), (1,))) * scale
            grad_probs = dot(v, grad, ((1,), (1,)))
            tanh = jnp.tanh(half_score)
            twice = 1.0 + tanh
            allowed = (where >= start - base) & (where <= pos - base)
            probs = jnp.where(allowed, half_score * twice, 0.0).astype(BF16)
            slope = twice * (1.0 + half_score * (1.0 - tanh))
            grad_scores = jnp.where(allowed, grad_probs * slope, 0.0).astype(BF16)
            here = pl.ds(pl.multiple_of(key_tile * rows, rows), rows)
            dv_ref[here, :] += dot(probs, grad, ((1,), (0,)))
            dk_ref[here, :] += dot(grad_scores, q, ((1,), (0,)))
            return total + dot(grad_scores, k, ((0,), (0,)))

        here = slice(tile * rows, (tile + 1) * rows)
        dq_ref[here, :] = lax.fori_loop(first_key_tile(tile, info), tile + 1, step, dq_ref[here, :])


def backward_other_kernel(info, mine_ref, other_ref, grad_ref, dq_ref, send_ref, gain_ref, dk_ref, dv_ref):
    dq_ref[...] = jnp.zeros_like(dq_ref)
    backward_tiles(info, mine_ref, other_ref, 0, 1 - info[0], grad_ref, dq_ref, dk_ref, dv_ref)
    send_ref[0] = (dk_ref[...] * (0.5 / math.sqrt(HEAD))).astype(BF16)
    send_ref[1] = dv_ref[...].astype(BF16)
    gain = jnp.zeros((EXTRA, HEAD), F32)
    for device in range(grad_ref.shape[0]):
        gain = gain + grad_ref[device, HALF : HALF + EXTRA, :].astype(F32)
    gain = jnp.sum(gain, axis=0, keepdims=True)
    gain_ref[...] = jnp.broadcast_to(gain[None], gain_ref.shape)


def backward_own_kernel(info, mine_ref, grad_ref, dq_in_ref, dq_ref, dk_ref, dv_ref):
    dq_ref[...] = dq_in_ref[...]
    backward_tiles(info, mine_ref, mine_ref, HALF, info[0], grad_ref, dq_ref, dk_ref, dv_ref)


def join_kernel(dq_ref, dk_ref, dv_ref, other_ref, gain_ref, out_ref):
    scale = 0.5 / math.sqrt(HEAD)
    gain = jnp.zeros(gain_ref.shape[1:], F32)
    for device in range(gain_ref.shape[0]):
        gain = gain + gain_ref[device]
    gain = in_three(gain[0:1])
    for slot in range(out_ref.shape[0]):
        here = slice(slot * HALF, (slot + 1) * HALF)
        out_ref[slot, 0:HALF, :] = (dq_ref[here, :] * scale).astype(BF16)
        dk = dk_ref[here, :] * scale + other_ref[0, here, :].astype(F32)
        out_ref[slot, HALF : 2 * HALF, :] = dk.astype(BF16)
        dv = dv_ref[here, :] + other_ref[1, here, :].astype(F32)
        out_ref[slot, 2 * HALF : 3 * HALF, :] = dv.astype(BF16)
        out_ref[slot, 3 * HALF : 3 * HALF + EXTRA, :] = gain


def unpack_kernel(in_ref, dq_ref, dk_ref, dv_ref, gain_ref):
    for device in range(in_ref.shape[0]):
        head, half = head_half(device)
        for part, ref in enumerate((dq_ref, dk_ref, dv_ref)):
            ref[half * HALF : (half + 1) * HALF, head * HEAD : (head + 1) * HEAD] = in_ref[
                device, part * HALF : (part + 1) * HALF, :
            ]
    for head in range(H):
        block = in_ref[2 * head, 3 * HALF : 3 * HALF + EXTRA, :].astype(F32)
        gain_ref[0:1, head * HEAD : (head + 1) * HEAD] = jnp.sum(block, axis=0, keepdims=True)


def call(kernel, outs, *args, scalars=0, scratch=(), flops=0):
    specs = [pl.BlockSpec(memory_space=pltpu.SMEM)] * scalars
    specs += [pl.BlockSpec(memory_space=pltpu.VMEM)] * (len(args) - scalars)
    moved = sum(math.prod(x.shape) * x.dtype.itemsize for x in list(args) + list(outs))
    return pl.pallas_call(
        kernel,
        out_shape=outs,
        in_specs=specs,
        out_specs=[pl.BlockSpec(memory_space=pltpu.VMEM)] * len(outs),
        scratch_shapes=scratch,
        compiler_params=pltpu.CompilerParams(vmem_limit_bytes=VMEM_LIMIT),
        cost_estimate=pl.CostEstimate(flops=flops, bytes_accessed=moved, transcendentals=flops // 512),
    )(*args)


def exchange(array, axis):
    return lax.all_to_all(array, axis, 0, 0, tiled=True)


def per_device(queries, keys, values, gates, lengths, gain, grad_out):
    rows, width = queries.shape[1:]
    devices = lax.axis_size("seq")
    groups = lax.axis_size("own")
    local = devices * HALF
    shape = jax.ShapeDtypeStruct
    me = lax.axis_index("seq")
    ends = jnp.cumsum(lengths[0])
    my_half = (me // 4) % 2
    info = jnp.concatenate([jnp.stack([my_half]), ends]).astype(jnp.int32)
    info_pos = jnp.concatenate([info, jnp.stack([me * rows])]).astype(jnp.int32)
    swap = [(device, device ^ 4) for device in range(devices)]
    work = 2 * local * local * HEAD // 2

    (packed,) = call(
        pack_kernel, [shape((devices, 3 * HALF, HEAD), BF16)], queries[0], keys[0], values[0]
    )
    mine = exchange(packed, "seq")
    other = lax.ppermute(mine[:, HALF:, :], "seq", swap)
    (own_sum,) = call(
        forward_own_kernel, [shape((local, HEAD), F32)], info, mine, scalars=1, flops=2 * work
    )
    (attended,) = call(
        forward_other_kernel,
        [shape((devices, HALF + EXTRA, HEAD), BF16)],
        info,
        mine,
        other,
        own_sum,
        scalars=1,
        flops=2 * work,
    )
    attended = exchange(attended, "seq")
    output, grad_gate, grad_att = call(
        norm_kernel,
        [
            shape((rows, width), BF16),
            shape((rows, width), BF16),
            shape((devices, HALF + EXTRA, HEAD), BF16),
        ],
        info_pos,
        attended,
        gates[0],
        grad_out[0],
        gain[None],
        scalars=1,
    )
    grad_att = exchange(grad_att, "seq")
    grad_sums = [pltpu.VMEM((local, HEAD), F32)] * 2
    dq, to_other, gain_part = call(
        backward_other_kernel,
        [
            shape((local, HEAD), F32),
            shape((2, local, HEAD), BF16),
            shape((groups, 8, HEAD), F32),
        ],
        info,
        mine,
        other,
        grad_att,
        scalars=1,
        scratch=grad_sums,
        flops=5 * work,
    )
    from_other = lax.ppermute(to_other, "seq", swap)
    gain_parts = exchange(gain_part, "own")
    dq, dk, dv = call(
        backward_own_kernel,
        [shape((local, HEAD), F32)] * 3,
        info,
        mine,
        grad_att,
        dq,
        scalars=1,
        flops=5 * work,
    )
    (joined,) = call(
        join_kernel,
        [shape((devices, 3 * HALF + EXTRA, HEAD), BF16)],
        dq,
        dk,
        dv,
        from_other,
        gain_parts,
    )
    grads = exchange(joined, "seq")
    grad_q, grad_k, grad_v, grad_gain = call(
        unpack_kernel,
        [shape((rows, width), BF16)] * 3 + [shape((1, width), F32)],
        grads,
    )
    return (output[None], grad_q[None], grad_k[None], grad_v[None], grad_gate[None], grad_gain[0])


def solution(mesh):
    wide = P("own", "seq", None)
    return jax.shard_map(
        per_device,
        mesh=mesh,
        in_specs=(wide, wide, wide, wide, P("own", None), P(), wide),
        out_specs=(wide, wide, wide, wide, wide, P()),
        check_vma=False,
    )
```

```python
import math

import jax
import jax.numpy as jnp
from jax import lax
from jax.experimental import pallas as pl
from jax.experimental.pallas import tpu as pltpu
from jax.sharding import PartitionSpec as P


H = 8
HEAD = 128
ZS = 4
ROWS = 128
PAIR = 2 * HEAD
TILE = 2 * ROWS
BLOCK = ZS * ROWS
EXTRA = 16
F32 = jnp.float32
BF16 = jnp.bfloat16
VMEM_LIMIT = 48 * 1024 * 1024


def dot(a, b, dims):
    return lax.dot_general(a, b, (dims, ((), ())), preferred_element_type=F32)


def iota(shape, dim):
    return lax.broadcasted_iota(jnp.int32, shape, dim)


def bounds(pos, info):
    start = jnp.zeros_like(pos)
    end = jnp.full_like(pos, 1 << 30)
    for user in range(info.shape[0] - 1):
        edge = info[1 + user]
        start = jnp.where(pos >= edge, jnp.maximum(start, edge), start)
        end = jnp.where(pos < edge, jnp.minimum(end, edge), end)
    return start, end - start


def head_cols(head):
    return slice(head * HEAD, (head + 1) * HEAD)


def tile_rows(ref, tile, first, head):
    block = ref[pl.ds(tile * 2, 2), first : first + ROWS, head_cols(head)]
    return block.reshape(TILE, HEAD)


def eye():
    return iota((ROWS, HEAD), 0) == iota((ROWS, HEAD), 1)


def to_row(column):
    return jnp.sum(jnp.where(eye(), column, 0.0), axis=0, keepdims=True)


def to_column(row):
    return jnp.sum(jnp.where(eye(), row, 0.0), axis=1, keepdims=True)


def pack_kv_kernel(k_ref, v_ref, out_ref):
    for z in range(ZS):
        cols = slice(z * PAIR, (z + 1) * PAIR)
        out_ref[z, 0:ROWS, :] = k_ref[:, cols]
        out_ref[z, ROWS : 2 * ROWS, :] = v_ref[:, cols]


def pack_q_kernel(q_ref, gates_ref, grad_ref, gain_ref, out_ref):
    for z in range(ZS):
        cols = slice(z * PAIR, (z + 1) * PAIR)
        out_ref[z, 0:ROWS, :] = q_ref[:, cols]
        dnorm = grad_ref[:, cols].astype(F32) * gates_ref[:, cols].astype(F32) * gain_ref[:, cols]
        out_ref[z, ROWS : 2 * ROWS, :] = dnorm.astype(BF16)


def key_tiles(info, tile, back):
    block = info[0] // ZS
    first, _ = bounds(block * BLOCK + tile * TILE, info)
    low = jnp.maximum(first // TILE - 2 * (block - back), 0)
    return low, (tile + 1 if back == 0 else 2)


def forward_kernel(info, qd_ref, kv0_ref, kv1_ref, kv2_ref, att_ref, stats_ref):
    scale = 0.5 / math.sqrt(HEAD)
    block = info[0] // ZS
    where = iota((1, TILE), 1)
    for tile in range(2):
        q = [tile_rows(qd_ref, tile, 0, head) for head in range(2)]
        pos = block * BLOCK + tile * TILE + iota((TILE, 1), 0)
        start, length = bounds(pos, info)
        total = (jnp.zeros((TILE, HEAD), F32),) * 2
        for back, kv_ref in enumerate((kv0_ref, kv1_ref, kv2_ref)):

            def step(key_tile, total):
                base = (block - back) * BLOCK + key_tile * TILE
                allowed = (where >= start - base) & (where <= pos - base)
                sums = []
                for head in range(2):
                    k = tile_rows(kv_ref, key_tile, 0, head)
                    v = tile_rows(kv_ref, key_tile, ROWS, head)
                    half_score = dot(q[head], k, ((1,), (1,))) * scale
                    silu = half_score + half_score * jnp.tanh(half_score)
                    probs = jnp.where(allowed, silu, 0.0).astype(BF16)
                    sums.append(total[head] + dot(probs, v, ((1,), (0,))))
                return tuple(sums)

            low, high = key_tiles(info, tile, back)
            total = lax.fori_loop(low, high, step, total)
        inverse = 1.0 / length.astype(F32)
        attended = [part * inverse for part in total]
        dnorm = [tile_rows(qd_ref, tile, ROWS, head).astype(F32) for head in range(2)]
        mean = jnp.sum(attended[0] + attended[1], axis=1, keepdims=True) / PAIR
        center = [part - mean for part in attended]
        square = jnp.sum(center[0] * center[0] + center[1] * center[1], axis=1, keepdims=True)
        plain = jnp.sum(dnorm[0] + dnorm[1], axis=1, keepdims=True)
        mixed = jnp.sum(dnorm[0] * center[0] + dnorm[1] * center[1], axis=1, keepdims=True)
        for part in range(2):
            span = slice(part * ROWS, (part + 1) * ROWS)
            slot = tile * 2 + part
            for index, column in enumerate((mean, square, plain, mixed)):
                row = to_row(column[span])
                for z in range(ZS):
                    stats_ref[z, index * ZS + slot : index * ZS + slot + 1, :] = row
        for head in range(2):
            att_ref[tile * TILE : (tile + 1) * TILE, head_cols(head)] = attended[head]


def part_cols(info, by, head):
    z = (info[0] - by) % ZS
    return pl.ds(pl.multiple_of(z * PAIR + head * HEAD, HEAD), HEAD)


def norm_kernel(info, in0_ref, in1_ref, in2_ref, in3_ref, *refs):
    gates_ref, grad_ref, gain_ref, out_ref, gate_grad_ref, gain_sum_ref = refs
    width = H * HEAD
    heads = [(by, ref, head) for by, ref in enumerate((in0_ref, in1_ref, in2_ref, in3_ref)) for head in range(2)]
    attended = []
    for by, ref, head in heads:
        mean = to_column(ref[ROWS : ROWS + 1, head_cols(head)].astype(F32))
        attended.append(ref[0:ROWS, head_cols(head)].astype(F32) + mean)
    mean = jnp.sum(sum(attended), axis=1, keepdims=True) / width
    center = [block - mean for block in attended]
    var = jnp.sum(sum(block * block for block in center), axis=1, keepdims=True) / width
    rstd = lax.rsqrt(var + 1e-05)
    for (by, ref, head), block in zip(heads, center):
        cols = part_cols(info, by, head)
        scaled = block * rstd * gain_ref[0:1, cols]
        out_ref[:, cols] = (scaled * gates_ref[:, cols].astype(F32)).astype(BF16)
        gate_grad_ref[:, cols] = (scaled * grad_ref[:, cols].astype(F32)).astype(BF16)
        three = ref[ROWS : ROWS + EXTRA, head_cols(head)].astype(F32)
        gain_sum_ref[0:1, cols] = three[1:2] + three[2:3] + three[3:4]


def make_grad_att(info, qd_ref, att_ref, stats_ref, grad_ref, gain_ref):
    width = H * HEAD
    block = info[0] // ZS
    sums = [jnp.zeros((1, HEAD), F32) for _ in range(2)]
    for slot in range(ZS):
        stat = [
            [stats_ref[z, index * ZS + slot : index * ZS + slot + 1, :] for z in range(ZS)]
            for index in range(4)
        ]
        means, squares, plains, mixeds = stat
        mean = sum(means) / ZS
        var = (sum(squares) + PAIR * sum((m - mean) * (m - mean) for m in means)) / width
        rstd = lax.rsqrt(var + 1e-05)
        first = sum(plains) / width
        second = rstd * sum(x + (m - mean) * p for x, m, p in zip(mixeds, means, plains)) / width
        _, length = bounds(block * BLOCK + slot * ROWS + iota((1, ROWS), 1), info)
        factor = rstd * (1.0 / length.astype(F32))
        mean, rstd, first, second, factor = (
            to_column(row) for row in (mean, rstd, first, second, factor)
        )
        rows = slice(slot * ROWS, (slot + 1) * ROWS)
        for head in range(2):
            normed = (att_ref[rows, head_cols(head)] - mean) * rstd
            dnorm = qd_ref[slot, ROWS : 2 * ROWS, head_cols(head)].astype(F32)
            sums[head] = sums[head] + jnp.sum(dnorm * normed, axis=0, keepdims=True)
            grad_att = factor * (dnorm - first - normed * second)
            grad_ref[slot, :, head_cols(head)] = grad_att.astype(BF16)
    for head in range(2):
        gain_ref[head : head + 1, :] = sums[head]


def make_back(info, att_ref, gain_ref, back_refs):
    index = iota((EXTRA, HEAD), 0)
    for head in range(2):
        cols = head_cols(head)
        gain = gain_ref[head : head + 1, :]
        high = gain.astype(BF16).astype(F32)
        mid = (gain - high).astype(BF16).astype(F32)
        low = gain - high - mid
        three = jnp.where(index == 1, high, jnp.where(index == 2, mid, low))
        for by, back_ref in enumerate(back_refs):
            slot = (info[0] + by) % ZS
            attended = att_ref[pl.ds(pl.multiple_of(slot * ROWS, ROWS), ROWS), cols]
            middle = jnp.mean(attended, axis=1, keepdims=True).astype(BF16).astype(F32)
            back_ref[0:ROWS, cols] = (attended - middle).astype(BF16)
            extra = jnp.where(index == 0, to_row(middle), three)
            back_ref[ROWS : ROWS + EXTRA, cols] = extra.astype(BF16)


def backward_tiles(info, back, q_ref, kv_ref, grad_ref, dq_ref, dkv_ref):
    scale = 0.5 / math.sqrt(HEAD)
    block = info[0] // ZS
    where = iota((TILE, 1), 0)
    dkv_ref[...] = jnp.zeros_like(dkv_ref)
    for tile in range(2):
        q = [tile_rows(q_ref, tile, 0, head) for head in range(2)]
        grad = [tile_rows(grad_ref, tile, 0, head) for head in range(2)]
        pos = block * BLOCK + tile * TILE + iota((1, TILE), 1)
        start, _ = bounds(pos, info)
        here = slice(tile * TILE, (tile + 1) * TILE)

        def step(key_tile, total):
            base = (block - back) * BLOCK + key_tile * TILE
            allowed = (where >= start - base) & (where <= pos - base)
            sums = []
            for head in range(2):
                k = tile_rows(kv_ref, key_tile, 0, head)
                v = tile_rows(kv_ref, key_tile, ROWS, head)
                half_score = dot(k, q[head], ((1,), (1,))) * scale
                grad_probs = dot(v, grad[head], ((1,), (1,)))
                tanh = jnp.tanh(half_score)
                twice = 1.0 + tanh
                probs = jnp.where(allowed, half_score * twice, 0.0).astype(BF16)
                slope = twice * (1.0 + half_score * (1.0 - tanh))
                grad_scores = jnp.where(allowed, grad_probs * slope, 0.0).astype(BF16)
                slots = pl.ds(key_tile * 2, 2)
                dk = dot(grad_scores, q[head], ((1,), (0,))).reshape(2, ROWS, HEAD)
                dv = dot(probs, grad[head], ((1,), (0,))).reshape(2, ROWS, HEAD)
                dkv_ref[slots, 0:ROWS, head_cols(head)] += dk
                dkv_ref[slots, ROWS : 2 * ROWS, head_cols(head)] += dv
                sums.append(total[head] + dot(grad_scores, k, ((0,), (0,))))
            return tuple(sums)

        low, high = key_tiles(info, tile, back)
        total = tuple(dq_ref[here, head_cols(head)] for head in range(2))
        total = lax.fori_loop(low, high, step, total)
        for head in range(2):
            dq_ref[here, head_cols(head)] = total[head]


def send_sums(dkv_ref, send_ref):
    scale = 0.5 / math.sqrt(HEAD)
    for slot in range(ZS):
        send_ref[slot, 0:ROWS, :] = (dkv_ref[slot, 0:ROWS, :] * scale).astype(BF16)
        send_ref[slot, ROWS : 2 * ROWS, :] = dkv_ref[slot, ROWS : 2 * ROWS, :].astype(BF16)


def backward_far_kernel(
    info, qd_ref, kv2_ref, att_ref, stats_ref, send_ref, grad_ref, dq_ref, gain_ref, dkv_ref
):
    make_grad_att(info, qd_ref, att_ref, stats_ref, grad_ref, gain_ref)
    dq_ref[...] = jnp.zeros_like(dq_ref)
    backward_tiles(info, 2, qd_ref, kv2_ref, grad_ref, dq_ref, dkv_ref)
    send_sums(dkv_ref, send_ref)


def backward_near_kernel(info, qd_ref, kv1_ref, grad_ref, dq_in_ref, send_ref, dq_ref, dkv_ref):
    dq_ref[...] = dq_in_ref[...]
    backward_tiles(info, 1, qd_ref, kv1_ref, grad_ref, dq_ref, dkv_ref)
    send_sums(dkv_ref, send_ref)


def backward_own_kernel(info, qd_ref, kv0_ref, grad_ref, att_ref, gain_ref, dq_in_ref, dq_ref, dkv_ref, *back_refs):
    make_back(info, att_ref, gain_ref, back_refs)
    dq_ref[...] = dq_in_ref[...]
    backward_tiles(info, 0, qd_ref, kv0_ref, grad_ref, dq_ref, dkv_ref)


def join_kernel(dq_ref, dkv_ref, other1_ref, other2_ref, out_ref):
    scale = 0.5 / math.sqrt(HEAD)
    for slot in range(ZS):
        others = other1_ref[slot].astype(F32) + other2_ref[slot].astype(F32)
        dk = dkv_ref[slot, 0:ROWS, :] * scale + others[0:ROWS]
        dv = dkv_ref[slot, ROWS : 2 * ROWS, :] + others[ROWS : 2 * ROWS]
        out_ref[slot, 0:ROWS, :] = dk.astype(BF16)
        out_ref[slot, ROWS : 2 * ROWS, :] = dv.astype(BF16)
        dq = dq_ref[slot * ROWS : (slot + 1) * ROWS, :] * scale
        out_ref[slot, 2 * ROWS : 3 * ROWS, :] = dq.astype(BF16)


def unpack_kernel(in_ref, dq_ref, dk_ref, dv_ref):
    for z in range(ZS):
        cols = slice(z * PAIR, (z + 1) * PAIR)
        dk_ref[:, cols] = in_ref[z, 0:ROWS, :]
        dv_ref[:, cols] = in_ref[z, ROWS : 2 * ROWS, :]
        dq_ref[:, cols] = in_ref[z, 2 * ROWS : 3 * ROWS, :]


def call(kernel, outs, *args, scalars=0, scratch=(), flops=1):
    specs = [pl.BlockSpec(memory_space=pltpu.SMEM)] * scalars
    specs += [pl.BlockSpec(memory_space=pltpu.VMEM)] * (len(args) - scalars)
    return pl.pallas_call(
        kernel,
        out_shape=outs,
        in_specs=specs,
        out_specs=[pl.BlockSpec(memory_space=pltpu.VMEM)] * len(outs),
        scratch_shapes=scratch,
        compiler_params=pltpu.CompilerParams(vmem_limit_bytes=VMEM_LIMIT),
        cost_estimate=pl.CostEstimate(flops=flops, bytes_accessed=0, transcendentals=0),
    )(*args)


def along_z(array):
    groups = [[y * ZS + z for z in range(ZS)] for y in range(ZS)]
    return lax.all_to_all(array, "seq", 0, 0, axis_index_groups=groups, tiled=True)


def shift_z(array, by):
    pairs = [(y * ZS + z, y * ZS + (z + by) % ZS) for y in range(ZS) for z in range(ZS)]
    return lax.ppermute(array, "seq", pairs)


def add_over(array, axis, bits):
    size = lax.axis_size(axis)
    for bit in bits:
        if bit < size:
            array = array + lax.ppermute(array, axis, [(i, i ^ bit) for i in range(size)])
    return array


def shift_y(array, by):
    devices = lax.axis_size("seq")
    pairs = [(i, i + ZS * by) for i in range(devices) if 0 <= i + ZS * by < devices]
    return lax.ppermute(array, "seq", pairs)


def per_device(queries, keys, values, gates, lengths, gain, grad_out):
    rows, width = queries.shape[1:]
    shape = jax.ShapeDtypeStruct
    ends = jnp.cumsum(lengths[0])
    info = jnp.concatenate([jnp.stack([lax.axis_index("seq")]), ends]).astype(jnp.int32)
    pair = shape((ZS, 2 * ROWS, PAIR), BF16)
    pair_sums = shape((ZS, 2 * ROWS, PAIR), F32)
    block = shape((BLOCK, PAIR), F32)
    sums_scratch = [pltpu.VMEM(pair_sums.shape, F32)]

    (kv,) = call(pack_kv_kernel, [pair], keys[0], values[0])
    kv0 = along_z(kv)
    kv2 = shift_y(kv0, 2)
    kv1 = shift_y(kv0, 1)
    (qd,) = call(pack_q_kernel, [pair], queries[0], gates[0], grad_out[0], gain[None])
    qd = along_z(qd)
    attended, stats = call(
        forward_kernel,
        [block, shape((ZS, 4 * ZS, ROWS), F32)],
        info,
        qd,
        kv0,
        kv1,
        kv2,
        scalars=1,
    )
    stats = along_z(stats)
    to2, grad_att, dq, gain_sum = call(
        backward_far_kernel,
        [pair, shape((ZS, ROWS, PAIR), BF16), block, shape((2, HEAD), F32)],
        info,
        qd,
        kv2,
        attended,
        stats,
        scalars=1,
        scratch=sums_scratch,
    )
    from2 = shift_y(to2, -2)
    to1, dq = call(
        backward_near_kernel,
        [pair, block],
        info,
        qd,
        kv1,
        grad_att,
        dq,
        scalars=1,
        scratch=sums_scratch,
    )
    from1 = shift_y(to1, -1)
    gain_sum, to1 = lax.optimization_barrier((gain_sum, to1))
    gain_sum = add_over(gain_sum, "own", (1,))
    dq, dkv, *back = call(
        backward_own_kernel,
        [block, pair_sums] + [shape((ROWS + EXTRA, PAIR), BF16)] * ZS,
        info,
        qd,
        kv0,
        grad_att,
        attended,
        gain_sum,
        dq,
        scalars=1,
    )
    back[2] = shift_z(back[2], 2)
    back[1] = shift_z(back[1], 1)
    back[3] = shift_z(back[3], 3)
    output, grad_gate, gain_sum = call(
        norm_kernel,
        [shape((rows, width), BF16)] * 2 + [shape((1, width), F32)],
        info,
        *back,
        gates[0],
        grad_out[0],
        gain[None],
        scalars=1,
    )
    (joined,) = call(join_kernel, [shape((ZS, 3 * ROWS, PAIR), BF16)], dq, dkv, from1, from2)
    gain_sum, joined = lax.optimization_barrier((gain_sum, joined))
    gain_sum = add_over(add_over(add_over(gain_sum, "own", (2, 4)), "seq", (4, 8)), "own", (8, 16))
    grad_gain = gain_sum.reshape(width) / gain
    grad_q, grad_k, grad_v = call(
        unpack_kernel, [shape((rows, width), BF16)] * 3, along_z(joined)
    )
    return (output[None], grad_q[None], grad_k[None], grad_v[None], grad_gate[None], grad_gain)


def solution(mesh):
    wide = P("own", "seq", None)
    return jax.shard_map(
        per_device,
        mesh=mesh,
        in_specs=(wide, wide, wide, wide, P("own", None), P(), wide),
        out_specs=(wide, wide, wide, wide, wide, P()),
        check_vma=False,
    )
```

```python
import math

import jax
import jax.numpy as jnp
from jax import lax
from jax.experimental import pallas as pl
from jax.experimental.pallas import tpu as pltpu
from jax.sharding import PartitionSpec as P


H = 8
HEAD = 128
ZS = 4
ROWS = 128
PAIR = 2 * HEAD
TILE = 2 * ROWS
BLOCK = ZS * ROWS
EXTRA = 16
F32 = jnp.float32
BF16 = jnp.bfloat16
VMEM_LIMIT = 48 * 1024 * 1024


def dot(a, b, dims):
    return lax.dot_general(a, b, (dims, ((), ())), preferred_element_type=F32)


def iota(shape, dim):
    return lax.broadcasted_iota(jnp.int32, shape, dim)


def bounds(pos, info):
    start = jnp.zeros_like(pos)
    end = jnp.full_like(pos, 1 << 30)
    for user in range(info.shape[0] - 1):
        edge = info[1 + user]
        start = jnp.where(pos >= edge, jnp.maximum(start, edge), start)
        end = jnp.where(pos < edge, jnp.minimum(end, edge), end)
    return start, end - start


def head_cols(head):
    return slice(head * HEAD, (head + 1) * HEAD)


def tile_rows(ref, tile, first, head, tiles=1):
    block = ref[pl.ds(tile * 2, 2 * tiles), first : first + ROWS, head_cols(head)]
    return block.reshape(tiles * TILE, HEAD)


def eye():
    return iota((ROWS, HEAD), 0) == iota((ROWS, HEAD), 1)


def to_row(column):
    return jnp.sum(jnp.where(eye(), column, 0.0), axis=0, keepdims=True)


def to_column(row):
    return jnp.sum(jnp.where(eye(), row, 0.0), axis=1, keepdims=True)


def pack_kv_kernel(k_ref, v_ref, out_ref, sems):
    copies = []
    for z in range(ZS):
        for part, ref in enumerate((k_ref, v_ref)):
            copies.append(
                pltpu.make_async_copy(
                    ref.at[:, z * PAIR : (z + 1) * PAIR],
                    out_ref.at[z, part * ROWS : (part + 1) * ROWS, :],
                    sems.at[2 * z + part],
                )
            )
    for copy in copies:
        copy.start()
    for copy in copies:
        copy.wait()


def pack_q_kernel(q_ref, gates_ref, grad_ref, gain_ref, out_ref):
    for z in range(ZS):
        cols = slice(z * PAIR, (z + 1) * PAIR)
        out_ref[z, 0:ROWS, :] = q_ref[:, cols]
        dnorm = grad_ref[:, cols].astype(F32) * gates_ref[:, cols].astype(F32) * gain_ref[:, cols]
        out_ref[z, ROWS : 2 * ROWS, :] = dnorm.astype(BF16)


def over_keys(info, tile, back, step, total):
    if back == 0:
        return step(0, tile + 1, total)
    block = info[0] // ZS
    first, _ = bounds(block * BLOCK + tile * TILE, info)
    low = jnp.clip(first // TILE - 2 * (block - back), 0, 2)
    return lax.switch(
        low, [lambda t: step(0, 2, t), lambda t: step(1, 1, t), lambda t: t], total
    )


def forward_tiles(info, tile, backs, qd_ref, kv_refs, total):
    scale = 0.5 / math.sqrt(HEAD)
    block = info[0] // ZS
    q = [tile_rows(qd_ref, tile, 0, head) for head in range(2)]
    pos = block * BLOCK + tile * TILE + iota((TILE, 1), 0)
    start, _ = bounds(pos, info)
    for back, kv_ref in zip(backs, kv_refs):

        def step(key_tile, tiles, total, back=back, kv_ref=kv_ref):
            base = (block - back) * BLOCK + key_tile * TILE
            where = iota((1, tiles * TILE), 1)
            allowed = (where >= start - base) & (where <= pos - base)
            sums = []
            for head in range(2):
                k = tile_rows(kv_ref, key_tile, 0, head, tiles)
                v = tile_rows(kv_ref, key_tile, ROWS, head, tiles)
                half_score = dot(q[head], k, ((1,), (1,))) * scale
                silu = half_score + half_score * jnp.tanh(half_score)
                probs = jnp.where(allowed, silu, 0.0).astype(BF16)
                sums.append(total[head] + dot(probs, v, ((1,), (0,))))
            return tuple(sums)

        total = over_keys(info, tile, back, step, total)
    return total


def forward_own_kernel(info, qd_ref, kv0_ref, sum_ref):
    for tile in range(2):
        total = (jnp.zeros((TILE, HEAD), F32),) * 2
        total = forward_tiles(info, tile, (0,), qd_ref, (kv0_ref,), total)
        for head in range(2):
            sum_ref[tile * TILE : (tile + 1) * TILE, head_cols(head)] = total[head]


def forward_kernel(info, qd_ref, kv1_ref, kv2_ref, sum_ref, att_ref, stats_ref):
    block = info[0] // ZS
    for tile in range(2):
        total = tuple(
            sum_ref[tile * TILE : (tile + 1) * TILE, head_cols(head)] for head in range(2)
        )
        total = forward_tiles(info, tile, (1, 2), qd_ref, (kv1_ref, kv2_ref), total)
        _, length = bounds(block * BLOCK + tile * TILE + iota((TILE, 1), 0), info)
        inverse = 1.0 / length.astype(F32)
        attended = [part * inverse for part in total]
        dnorm = [tile_rows(qd_ref, tile, ROWS, head).astype(F32) for head in range(2)]
        mean = jnp.sum(attended[0] + attended[1], axis=1, keepdims=True) / PAIR
        center = [part - mean for part in attended]
        square = jnp.sum(center[0] * center[0] + center[1] * center[1], axis=1, keepdims=True)
        plain = jnp.sum(dnorm[0] + dnorm[1], axis=1, keepdims=True)
        mixed = jnp.sum(dnorm[0] * center[0] + dnorm[1] * center[1], axis=1, keepdims=True)
        for part in range(2):
            span = slice(part * ROWS, (part + 1) * ROWS)
            slot = tile * 2 + part
            for index, column in enumerate((mean, square, plain, mixed)):
                row = to_row(column[span])
                for z in range(ZS):
                    stats_ref[z, index * ZS + slot : index * ZS + slot + 1, :] = row
        for head in range(2):
            att_ref[tile * TILE : (tile + 1) * TILE, head_cols(head)] = attended[head]


def part_cols(info, by, head):
    z = (info[0] - by) % ZS
    return pl.ds(pl.multiple_of(z * PAIR + head * HEAD, HEAD), HEAD)


def norm_kernel(info, in0_ref, in1_ref, in2_ref, in3_ref, *refs):
    gates_ref, grad_ref, gain_ref, out_ref, gate_grad_ref = refs
    width = H * HEAD
    heads = [(by, ref, head) for by, ref in enumerate((in0_ref, in1_ref, in2_ref, in3_ref)) for head in range(2)]
    attended = []
    for by, ref, head in heads:
        mean = to_column(ref[ROWS : ROWS + 1, head_cols(head)].astype(F32))
        attended.append(ref[0:ROWS, head_cols(head)].astype(F32) + mean)
    mean = jnp.sum(sum(attended), axis=1, keepdims=True) / width
    center = [block - mean for block in attended]
    var = jnp.sum(sum(block * block for block in center), axis=1, keepdims=True) / width
    rstd = lax.rsqrt(var + 1e-05)
    for (by, ref, head), block in zip(heads, center):
        cols = part_cols(info, by, head)
        scaled = block * rstd * gain_ref[0:1, cols]
        out_ref[:, cols] = (scaled * gates_ref[:, cols].astype(F32)).astype(BF16)
        gate_grad_ref[:, cols] = (scaled * grad_ref[:, cols].astype(F32)).astype(BF16)


def gain_kernel(info, in0_ref, in1_ref, in2_ref, in3_ref, sum_ref):
    for by, ref in enumerate((in0_ref, in1_ref, in2_ref, in3_ref)):
        for head in range(2):
            three = ref[ROWS : ROWS + EXTRA, head_cols(head)].astype(F32)
            sum_ref[0:1, part_cols(info, by, head)] = three[1:2] + three[2:3] + three[3:4]


def make_grad_att(info, qd_ref, att_ref, stats_ref, grad_ref, gain_ref):
    width = H * HEAD
    block = info[0] // ZS
    sums = [jnp.zeros((1, HEAD), F32) for _ in range(2)]
    for slot in range(ZS):
        stat = [
            [stats_ref[z, index * ZS + slot : index * ZS + slot + 1, :] for z in range(ZS)]
            for index in range(4)
        ]
        means, squares, plains, mixeds = stat
        mean = sum(means) / ZS
        var = (sum(squares) + PAIR * sum((m - mean) * (m - mean) for m in means)) / width
        rstd = lax.rsqrt(var + 1e-05)
        first = sum(plains) / width
        second = rstd * sum(x + (m - mean) * p for x, m, p in zip(mixeds, means, plains)) / width
        _, length = bounds(block * BLOCK + slot * ROWS + iota((1, ROWS), 1), info)
        factor = rstd * (1.0 / length.astype(F32))
        mean, rstd, first, second, factor = (
            to_column(row) for row in (mean, rstd, first, second, factor)
        )
        rows = slice(slot * ROWS, (slot + 1) * ROWS)
        for head in range(2):
            normed = (att_ref[rows, head_cols(head)] - mean) * rstd
            dnorm = qd_ref[slot, ROWS : 2 * ROWS, head_cols(head)].astype(F32)
            sums[head] = sums[head] + jnp.sum(dnorm * normed, axis=0, keepdims=True)
            grad_att = factor * (dnorm - first - normed * second)
            grad_ref[slot, :, head_cols(head)] = grad_att.astype(BF16)
    for head in range(2):
        gain_ref[head : head + 1, :] = sums[head]


def back_kernel(info, att_ref, gain_ref, *back_refs):
    index = iota((EXTRA, HEAD), 0)
    for head in range(2):
        cols = head_cols(head)
        gain = gain_ref[head : head + 1, :]
        high = gain.astype(BF16).astype(F32)
        mid = (gain - high).astype(BF16).astype(F32)
        low = gain - high - mid
        three = jnp.where(index == 1, high, jnp.where(index == 2, mid, low))
        for by, back_ref in enumerate(back_refs):
            slot = (info[0] + by) % ZS
            attended = att_ref[pl.ds(pl.multiple_of(slot * ROWS, ROWS), ROWS), cols]
            middle = jnp.mean(attended, axis=1, keepdims=True).astype(BF16).astype(F32)
            back_ref[0:ROWS, cols] = (attended - middle).astype(BF16)
            extra = jnp.where(index == 0, to_row(middle), three)
            back_ref[ROWS : ROWS + EXTRA, cols] = extra.astype(BF16)


def backward_tiles(info, back, q_ref, kv_ref, grad_ref, dq_ref, dkv_ref):
    scale = 0.5 / math.sqrt(HEAD)
    block = info[0] // ZS
    dkv_ref[...] = jnp.zeros_like(dkv_ref)
    for tile in range(2):
        q = [tile_rows(q_ref, tile, 0, head) for head in range(2)]
        grad = [tile_rows(grad_ref, tile, 0, head) for head in range(2)]
        pos = block * BLOCK + tile * TILE + iota((1, TILE), 1)
        start, _ = bounds(pos, info)
        here = slice(tile * TILE, (tile + 1) * TILE)

        def step(key_tile, tiles, total):
            base = (block - back) * BLOCK + key_tile * TILE
            where = iota((tiles * TILE, 1), 0)
            allowed = (where >= start - base) & (where <= pos - base)
            sums = []
            for head in range(2):
                k = tile_rows(kv_ref, key_tile, 0, head, tiles)
                v = tile_rows(kv_ref, key_tile, ROWS, head, tiles)
                half_score = dot(k, q[head], ((1,), (1,))) * scale
                grad_probs = dot(v, grad[head], ((1,), (1,)))
                tanh = jnp.tanh(half_score)
                twice = 1.0 + tanh
                probs = jnp.where(allowed, half_score * twice, 0.0).astype(BF16)
                slope = twice * (1.0 + half_score * (1.0 - tanh))
                grad_scores = jnp.where(allowed, grad_probs * slope, 0.0).astype(BF16)
                slots = pl.ds(key_tile * 2, 2 * tiles)
                dk = dot(grad_scores, q[head], ((1,), (0,))).reshape(2 * tiles, ROWS, HEAD)
                dv = dot(probs, grad[head], ((1,), (0,))).reshape(2 * tiles, ROWS, HEAD)
                dkv_ref[slots, 0:ROWS, head_cols(head)] += dk
                dkv_ref[slots, ROWS : 2 * ROWS, head_cols(head)] += dv
                sums.append(total[head] + dot(grad_scores, k, ((0,), (0,))))
            return tuple(sums)

        total = tuple(dq_ref[here, head_cols(head)] for head in range(2))
        total = over_keys(info, tile, back, step, total)
        for head in range(2):
            dq_ref[here, head_cols(head)] = total[head]


def send_sums(dkv_ref, send_ref):
    scale = 0.5 / math.sqrt(HEAD)
    for slot in range(ZS):
        send_ref[slot, 0:ROWS, :] = (dkv_ref[slot, 0:ROWS, :] * scale).astype(BF16)
        send_ref[slot, ROWS : 2 * ROWS, :] = dkv_ref[slot, ROWS : 2 * ROWS, :].astype(BF16)


def backward_far_kernel(
    info, qd_ref, kv2_ref, att_ref, stats_ref, send_ref, grad_ref, dq_ref, gain_ref, dkv_ref
):
    make_grad_att(info, qd_ref, att_ref, stats_ref, grad_ref, gain_ref)
    dq_ref[...] = jnp.zeros_like(dq_ref)
    backward_tiles(info, 2, qd_ref, kv2_ref, grad_ref, dq_ref, dkv_ref)
    send_sums(dkv_ref, send_ref)


def backward_near_kernel(info, qd_ref, kv1_ref, grad_ref, dq_in_ref, send_ref, dq_ref, dkv_ref):
    dq_ref[...] = dq_in_ref[...]
    backward_tiles(info, 1, qd_ref, kv1_ref, grad_ref, dq_ref, dkv_ref)
    send_sums(dkv_ref, send_ref)


def backward_own_kernel(info, qd_ref, kv0_ref, grad_ref, dq_in_ref, dq_ref, dkv_ref):
    dq_ref[...] = dq_in_ref[...]
    backward_tiles(info, 0, qd_ref, kv0_ref, grad_ref, dq_ref, dkv_ref)


def join_kernel(dq_ref, dkv_ref, other1_ref, other2_ref, out_ref):
    scale = 0.5 / math.sqrt(HEAD)
    for slot in range(ZS):
        others = other1_ref[slot].astype(F32) + other2_ref[slot].astype(F32)
        dk = dkv_ref[slot, 0:ROWS, :] * scale + others[0:ROWS]
        dv = dkv_ref[slot, ROWS : 2 * ROWS, :] + others[ROWS : 2 * ROWS]
        out_ref[slot, 0:ROWS, :] = dk.astype(BF16)
        out_ref[slot, ROWS : 2 * ROWS, :] = dv.astype(BF16)
        dq = dq_ref[slot * ROWS : (slot + 1) * ROWS, :] * scale
        out_ref[slot, 2 * ROWS : 3 * ROWS, :] = dq.astype(BF16)


def unpack_kernel(in_ref, gain_sum_ref, gain_ref, dq_ref, dk_ref, dv_ref, grad_gain_ref):
    grad_gain_ref[...] = gain_sum_ref[...] / gain_ref[...]
    for z in range(ZS):
        cols = slice(z * PAIR, (z + 1) * PAIR)
        dk_ref[:, cols] = in_ref[z, 0:ROWS, :]
        dv_ref[:, cols] = in_ref[z, ROWS : 2 * ROWS, :]
        dq_ref[:, cols] = in_ref[z, 2 * ROWS : 3 * ROWS, :]


def call(kernel, outs, *args, scalars=0, scratch=(), flops=1, space=pltpu.VMEM):
    specs = [pl.BlockSpec(memory_space=pltpu.SMEM)] * scalars
    specs += [pl.BlockSpec(memory_space=space)] * (len(args) - scalars)
    return pl.pallas_call(
        kernel,
        out_shape=outs,
        in_specs=specs,
        out_specs=[pl.BlockSpec(memory_space=pltpu.VMEM)] * len(outs),
        scratch_shapes=scratch,
        compiler_params=pltpu.CompilerParams(vmem_limit_bytes=VMEM_LIMIT),
        cost_estimate=pl.CostEstimate(flops=flops, bytes_accessed=0, transcendentals=0),
    )(*args)


def along_z(array):
    groups = [[y * ZS + z for z in range(ZS)] for y in range(ZS)]
    return lax.all_to_all(array, "seq", 0, 0, axis_index_groups=groups, tiled=True)


def shift_z(array, by):
    pairs = [(y * ZS + z, y * ZS + (z + by) % ZS) for y in range(ZS) for z in range(ZS)]
    return lax.ppermute(array, "seq", pairs)


def add_over(array, axis, low):
    size = lax.axis_size(axis)
    if 2 * low >= size:
        return array
    others = [
        lax.ppermute(array, axis, [(i, i ^ bits) for i in range(size)])
        for bits in (low, 2 * low, 3 * low)
    ]
    return (array + others[0]) + (others[1] + others[2])


def add_pairs(array, axis):
    size = lax.axis_size(axis)
    if size == 1:
        return array
    return array + lax.ppermute(array, axis, [(i, i ^ 1) for i in range(size)])


def shift_y(array, by):
    devices = lax.axis_size("seq")
    pairs = [(i, i + ZS * by) for i in range(devices) if 0 <= i + ZS * by < devices]
    return lax.ppermute(array, "seq", pairs)


def per_device(queries, keys, values, gates, lengths, gain, grad_out):
    rows, width = queries.shape[1:]
    shape = jax.ShapeDtypeStruct
    ends = jnp.cumsum(lengths[0])
    info = jnp.concatenate([jnp.stack([lax.axis_index("seq")]), ends]).astype(jnp.int32)
    pair = shape((ZS, 2 * ROWS, PAIR), BF16)
    pair_sums = shape((ZS, 2 * ROWS, PAIR), F32)
    block = shape((BLOCK, PAIR), F32)
    sums_scratch = [pltpu.VMEM(pair_sums.shape, F32)]

    (kv,) = call(
        pack_kv_kernel,
        [pair],
        keys[0],
        values[0],
        space=pltpu.HBM,
        scratch=[pltpu.SemaphoreType.DMA((2 * ZS,))],
    )
    kv0 = along_z(kv)
    kv2 = shift_y(kv0, 2)
    kv1 = shift_y(kv0, 1)
    (qd,) = call(pack_q_kernel, [pair], queries[0], gates[0], grad_out[0], gain[None])
    qd = along_z(qd)
    (own_sum,) = call(forward_own_kernel, [block], info, qd, kv0, scalars=1)
    attended, stats = call(
        forward_kernel,
        [block, shape((ZS, 4 * ZS, ROWS), F32)],
        info,
        qd,
        kv1,
        kv2,
        own_sum,
        scalars=1,
    )
    stats = along_z(stats)
    to2, grad_att, dq, gain_sum = call(
        backward_far_kernel,
        [pair, shape((ZS, ROWS, PAIR), BF16), block, shape((2, HEAD), F32)],
        info,
        qd,
        kv2,
        attended,
        stats,
        scalars=1,
        scratch=sums_scratch,
    )
    from2 = shift_y(to2, -2)
    to1, dq = call(
        backward_near_kernel,
        [pair, block],
        info,
        qd,
        kv1,
        grad_att,
        dq,
        scalars=1,
        scratch=sums_scratch,
    )
    from1 = shift_y(to1, -1)
    gain_sum, to1 = lax.optimization_barrier((gain_sum, to1))
    back = call(
        back_kernel,
        [shape((ROWS + EXTRA, PAIR), BF16)] * ZS,
        info,
        attended,
        gain_sum,
        scalars=1,
    )
    back = list(back)
    back[2] = shift_z(back[2], 2)
    back[1] = shift_z(back[1], 1)
    back[3] = shift_z(back[3], 3)
    dq, dkv = call(
        backward_own_kernel, [block, pair_sums], info, qd, kv0, grad_att, dq, scalars=1
    )
    (gain_sum,) = call(gain_kernel, [shape((1, width), F32)], info, *back, scalars=1)
    output, grad_gate = call(
        norm_kernel,
        [shape((rows, width), BF16)] * 2,
        info,
        *back,
        gates[0],
        grad_out[0],
        gain[None],
        scalars=1,
    )
    (joined,) = call(join_kernel, [shape((ZS, 3 * ROWS, PAIR), BF16)], dq, dkv, from1, from2)
    gain_sum, joined = lax.optimization_barrier((gain_sum, joined))
    gain_sum = add_pairs(gain_sum, "own")
    gain_sum = add_over(add_over(add_over(gain_sum, "own", 2), "seq", 4), "own", 8)
    grad_q, grad_k, grad_v, grad_gain = call(
        unpack_kernel,
        [shape((rows, width), BF16)] * 3 + [shape((1, width), F32)],
        along_z(joined),
        gain_sum,
        gain[None],
    )
    return (output[None], grad_q[None], grad_k[None], grad_v[None], grad_gate[None], grad_gain[0])


def solution(mesh):
    wide = P("own", "seq", None)
    return jax.shard_map(
        per_device,
        mesh=mesh,
        in_specs=(wide, wide, wide, wide, P("own", None), P(), wide),
        out_specs=(wide, wide, wide, wide, wide, P()),
        check_vma=False,
    )
```

```python
import math

import jax
import jax.numpy as jnp
from jax import lax
from jax.experimental import pallas as pl
from jax.experimental.pallas import tpu as pltpu
from jax.sharding import PartitionSpec as P


H = 8
HEAD = 128
ZS = 4
ROWS = 128
PAIR = 2 * HEAD
TILE = 2 * ROWS
BLOCK = ZS * ROWS
EXTRA = 16
F32 = jnp.float32
BF16 = jnp.bfloat16
VMEM_LIMIT = 48 * 1024 * 1024


def dot(a, b, dims):
    return lax.dot_general(a, b, (dims, ((), ())), preferred_element_type=F32)


def iota(shape, dim):
    return lax.broadcasted_iota(jnp.int32, shape, dim)


def bounds(pos, info):
    start = jnp.zeros_like(pos)
    end = jnp.full_like(pos, 1 << 30)
    for user in range(info.shape[0] - 1):
        edge = info[1 + user]
        start = jnp.where(pos >= edge, jnp.maximum(start, edge), start)
        end = jnp.where(pos < edge, jnp.minimum(end, edge), end)
    return start, end - start


def head_cols(head):
    return slice(head * HEAD, (head + 1) * HEAD)


def tile_rows(ref, tile, first, head, tiles=1):
    block = ref[pl.ds(tile * 2, 2 * tiles), first : first + ROWS, head_cols(head)]
    return block.reshape(tiles * TILE, HEAD)


def eye():
    return iota((ROWS, HEAD), 0) == iota((ROWS, HEAD), 1)


def to_row(column):
    return jnp.sum(jnp.where(eye(), column, 0.0), axis=0, keepdims=True)


def to_column(row):
    return jnp.sum(jnp.where(eye(), row, 0.0), axis=1, keepdims=True)


def pack_kv_kernel(k_ref, v_ref, out_ref, sems):
    copies = []
    for z in range(ZS):
        for part, ref in enumerate((k_ref, v_ref)):
            copies.append(
                pltpu.make_async_copy(
                    ref.at[:, z * PAIR : (z + 1) * PAIR],
                    out_ref.at[z, part * ROWS : (part + 1) * ROWS, :],
                    sems.at[2 * z + part],
                )
            )
    for copy in copies:
        copy.start()
    for copy in copies:
        copy.wait()


def pack_q_kernel(q_ref, gates_ref, grad_ref, gain_ref, out_ref):
    for z in range(ZS):
        cols = slice(z * PAIR, (z + 1) * PAIR)
        out_ref[z, 0:ROWS, :] = q_ref[:, cols]
        dnorm = grad_ref[:, cols].astype(F32) * gates_ref[:, cols].astype(F32) * gain_ref[:, cols]
        out_ref[z, ROWS : 2 * ROWS, :] = dnorm.astype(BF16)


def over_keys(info, tile, back, step, total):
    if back == 0:
        return step(0, tile + 1, total)
    block = info[0] // ZS
    first, _ = bounds(block * BLOCK + tile * TILE, info)
    low = jnp.clip(first // TILE - 2 * (block - back), 0, 2)
    return lax.switch(
        low, [lambda t: step(0, 2, t), lambda t: step(1, 1, t), lambda t: t], total
    )


def forward_tiles(info, tile, backs, qd_ref, kv_refs, total):
    scale = 0.5 / math.sqrt(HEAD)
    block = info[0] // ZS
    q = [tile_rows(qd_ref, tile, 0, head) for head in range(2)]
    pos = block * BLOCK + tile * TILE + iota((TILE, 1), 0)
    start, _ = bounds(pos, info)
    for back, kv_ref in zip(backs, kv_refs):

        def step(key_tile, tiles, total, back=back, kv_ref=kv_ref):
            base = (block - back) * BLOCK + key_tile * TILE
            where = iota((1, tiles * TILE), 1)
            allowed = where >= start - base
            if back == 0:
                allowed = allowed & (where <= pos - base)
            sums = []
            for head in range(2):
                k = tile_rows(kv_ref, key_tile, 0, head, tiles)
                v = tile_rows(kv_ref, key_tile, ROWS, head, tiles)
                half_score = dot(q[head], k, ((1,), (1,))) * scale
                silu = half_score + half_score * jnp.tanh(half_score)
                probs = jnp.where(allowed, silu, 0.0).astype(BF16)
                sums.append(total[head] + dot(probs, v, ((1,), (0,))))
            return tuple(sums)

        total = over_keys(info, tile, back, step, total)
    return total


def forward_own_kernel(info, qd_ref, kv0_ref, sum_ref):
    for tile in range(2):
        total = (jnp.zeros((TILE, HEAD), F32),) * 2
        total = forward_tiles(info, tile, (0,), qd_ref, (kv0_ref,), total)
        for head in range(2):
            sum_ref[tile * TILE : (tile + 1) * TILE, head_cols(head)] = total[head]


def forward_kernel(info, qd_ref, kv1_ref, kv2_ref, sum_ref, att_ref, stats_ref):
    block = info[0] // ZS
    for tile in range(2):
        total = tuple(
            sum_ref[tile * TILE : (tile + 1) * TILE, head_cols(head)] for head in range(2)
        )
        total = forward_tiles(info, tile, (1, 2), qd_ref, (kv1_ref, kv2_ref), total)
        _, length = bounds(block * BLOCK + tile * TILE + iota((TILE, 1), 0), info)
        inverse = 1.0 / length.astype(F32)
        attended = [part * inverse for part in total]
        dnorm = [tile_rows(qd_ref, tile, ROWS, head).astype(F32) for head in range(2)]
        mean = jnp.sum(attended[0] + attended[1], axis=1, keepdims=True) / PAIR
        center = [part - mean for part in attended]
        square = jnp.sum(center[0] * center[0] + center[1] * center[1], axis=1, keepdims=True)
        plain = jnp.sum(dnorm[0] + dnorm[1], axis=1, keepdims=True)
        mixed = jnp.sum(dnorm[0] * center[0] + dnorm[1] * center[1], axis=1, keepdims=True)
        for part in range(2):
            span = slice(part * ROWS, (part + 1) * ROWS)
            slot = tile * 2 + part
            for index, column in enumerate((mean, square, plain, mixed)):
                row = to_row(column[span])
                for z in range(ZS):
                    stats_ref[z, index * ZS + slot : index * ZS + slot + 1, :] = row
        for head in range(2):
            att_ref[tile * TILE : (tile + 1) * TILE, head_cols(head)] = attended[head]


def part_cols(info, by, head):
    z = (info[0] - by) % ZS
    return pl.ds(pl.multiple_of(z * PAIR + head * HEAD, HEAD), HEAD)


def norm_kernel(info, in0_ref, in1_ref, in2_ref, in3_ref, *refs):
    gates_ref, grad_ref, gain_ref, out_ref, gate_grad_ref = refs
    width = H * HEAD
    heads = [(by, ref, head) for by, ref in enumerate((in0_ref, in1_ref, in2_ref, in3_ref)) for head in range(2)]
    attended = []
    for by, ref, head in heads:
        mean = to_column(ref[ROWS : ROWS + 1, head_cols(head)].astype(F32))
        attended.append(ref[0:ROWS, head_cols(head)].astype(F32) + mean)
    mean = jnp.sum(sum(attended), axis=1, keepdims=True) / width
    center = [block - mean for block in attended]
    var = jnp.sum(sum(block * block for block in center), axis=1, keepdims=True) / width
    rstd = lax.rsqrt(var + 1e-05)
    for (by, ref, head), block in zip(heads, center):
        cols = part_cols(info, by, head)
        scaled = block * rstd * gain_ref[0:1, cols]
        out_ref[:, cols] = (scaled * gates_ref[:, cols].astype(F32)).astype(BF16)
        gate_grad_ref[:, cols] = (scaled * grad_ref[:, cols].astype(F32)).astype(BF16)


def gain_kernel(info, in0_ref, in1_ref, in2_ref, in3_ref, sum_ref):
    for by, ref in enumerate((in0_ref, in1_ref, in2_ref, in3_ref)):
        for head in range(2):
            three = ref[ROWS : ROWS + EXTRA, head_cols(head)].astype(F32)
            sum_ref[0:1, part_cols(info, by, head)] = three[1:2] + three[2:3] + three[3:4]


def make_grad_att(info, qd_ref, att_ref, stats_ref, grad_ref, gain_ref):
    width = H * HEAD
    block = info[0] // ZS
    sums = [jnp.zeros((1, HEAD), F32) for _ in range(2)]
    for slot in range(ZS):
        stat = [
            [stats_ref[z, index * ZS + slot : index * ZS + slot + 1, :] for z in range(ZS)]
            for index in range(4)
        ]
        means, squares, plains, mixeds = stat
        mean = sum(means) / ZS
        var = (sum(squares) + PAIR * sum((m - mean) * (m - mean) for m in means)) / width
        rstd = lax.rsqrt(var + 1e-05)
        first = sum(plains) / width
        second = rstd * sum(x + (m - mean) * p for x, m, p in zip(mixeds, means, plains)) / width
        _, length = bounds(block * BLOCK + slot * ROWS + iota((1, ROWS), 1), info)
        factor = rstd * (1.0 / length.astype(F32))
        mean, rstd, first, second, factor = (
            to_column(row) for row in (mean, rstd, first, second, factor)
        )
        rows = slice(slot * ROWS, (slot + 1) * ROWS)
        for head in range(2):
            normed = (att_ref[rows, head_cols(head)] - mean) * rstd
            dnorm = qd_ref[slot, ROWS : 2 * ROWS, head_cols(head)].astype(F32)
            sums[head] = sums[head] + jnp.sum(dnorm * normed, axis=0, keepdims=True)
            grad_att = factor * (dnorm - first - normed * second)
            grad_ref[slot, :, head_cols(head)] = grad_att.astype(BF16)
    for head in range(2):
        gain_ref[head : head + 1, :] = sums[head]


def back_kernel(info, att_ref, gain_ref, *back_refs):
    index = iota((EXTRA, HEAD), 0)
    for head in range(2):
        cols = head_cols(head)
        gain = gain_ref[head : head + 1, :]
        high = gain.astype(BF16).astype(F32)
        mid = (gain - high).astype(BF16).astype(F32)
        low = gain - high - mid
        three = jnp.where(index == 1, high, jnp.where(index == 2, mid, low))
        for by, back_ref in enumerate(back_refs):
            slot = (info[0] + by) % ZS
            attended = att_ref[pl.ds(pl.multiple_of(slot * ROWS, ROWS), ROWS), cols]
            middle = jnp.mean(attended, axis=1, keepdims=True).astype(BF16).astype(F32)
            back_ref[0:ROWS, cols] = (attended - middle).astype(BF16)
            extra = jnp.where(index == 0, to_row(middle), three)
            back_ref[ROWS : ROWS + EXTRA, cols] = extra.astype(BF16)


def backward_tiles(info, back, q_ref, kv_ref, grad_ref, dq_ref, dkv_ref):
    scale = 0.5 / math.sqrt(HEAD)
    block = info[0] // ZS
    dkv_ref[...] = jnp.zeros_like(dkv_ref)
    for tile in range(2):
        q = [tile_rows(q_ref, tile, 0, head) for head in range(2)]
        grad = [tile_rows(grad_ref, tile, 0, head) for head in range(2)]
        pos = block * BLOCK + tile * TILE + iota((1, TILE), 1)
        start, _ = bounds(pos, info)
        here = slice(tile * TILE, (tile + 1) * TILE)

        def step(key_tile, tiles, total):
            base = (block - back) * BLOCK + key_tile * TILE
            where = iota((tiles * TILE, 1), 0)
            allowed = where >= start - base
            if back == 0:
                allowed = allowed & (where <= pos - base)
            sums = []
            for head in range(2):
                k = tile_rows(kv_ref, key_tile, 0, head, tiles)
                v = tile_rows(kv_ref, key_tile, ROWS, head, tiles)
                half_score = dot(k, q[head], ((1,), (1,))) * scale
                grad_probs = dot(v, grad[head], ((1,), (1,)))
                tanh = jnp.tanh(half_score)
                twice = 1.0 + tanh
                probs = jnp.where(allowed, half_score * twice, 0.0).astype(BF16)
                slope = twice * (1.0 + half_score * (1.0 - tanh))
                grad_scores = jnp.where(allowed, grad_probs * slope, 0.0).astype(BF16)
                slots = pl.ds(key_tile * 2, 2 * tiles)
                dk = dot(grad_scores, q[head], ((1,), (0,))).reshape(2 * tiles, ROWS, HEAD)
                dv = dot(probs, grad[head], ((1,), (0,))).reshape(2 * tiles, ROWS, HEAD)
                dkv_ref[slots, 0:ROWS, head_cols(head)] += dk
                dkv_ref[slots, ROWS : 2 * ROWS, head_cols(head)] += dv
                sums.append(total[head] + dot(k, grad_scores, ((0,), (0,))))
            return tuple(sums)

        total = tuple(dq_ref[head_cols(head), here] for head in range(2))
        total = over_keys(info, tile, back, step, total)
        for head in range(2):
            dq_ref[head_cols(head), here] = total[head]


def send_sums(dkv_ref, send_ref):
    scale = 0.5 / math.sqrt(HEAD)
    for slot in range(ZS):
        send_ref[slot, 0:ROWS, :] = (dkv_ref[slot, 0:ROWS, :] * scale).astype(BF16)
        send_ref[slot, ROWS : 2 * ROWS, :] = dkv_ref[slot, ROWS : 2 * ROWS, :].astype(BF16)


def backward_far_kernel(
    info, qd_ref, kv2_ref, att_ref, stats_ref, send_ref, grad_ref, dq_ref, gain_ref, dkv_ref
):
    make_grad_att(info, qd_ref, att_ref, stats_ref, grad_ref, gain_ref)
    dq_ref[...] = jnp.zeros_like(dq_ref)
    backward_tiles(info, 2, qd_ref, kv2_ref, grad_ref, dq_ref, dkv_ref)
    send_sums(dkv_ref, send_ref)


def backward_near_kernel(info, qd_ref, kv1_ref, grad_ref, dq_in_ref, send_ref, dq_ref, dkv_ref):
    dq_ref[...] = dq_in_ref[...]
    backward_tiles(info, 1, qd_ref, kv1_ref, grad_ref, dq_ref, dkv_ref)
    send_sums(dkv_ref, send_ref)


def backward_own_kernel(info, qd_ref, kv0_ref, grad_ref, dq_in_ref, dq_ref, dkv_ref):
    dq_ref[...] = dq_in_ref[...]
    backward_tiles(info, 0, qd_ref, kv0_ref, grad_ref, dq_ref, dkv_ref)


def join_kernel(dq_ref, dkv_ref, other1_ref, other2_ref, out_ref):
    scale = 0.5 / math.sqrt(HEAD)
    for slot in range(ZS):
        others = other1_ref[slot].astype(F32) + other2_ref[slot].astype(F32)
        dk = dkv_ref[slot, 0:ROWS, :] * scale + others[0:ROWS]
        dv = dkv_ref[slot, ROWS : 2 * ROWS, :] + others[ROWS : 2 * ROWS]
        out_ref[slot, 0:ROWS, :] = dk.astype(BF16)
        out_ref[slot, ROWS : 2 * ROWS, :] = dv.astype(BF16)
        for head in range(2):
            dq = dq_ref[head_cols(head), slot * ROWS : (slot + 1) * ROWS].T * scale
            out_ref[slot, 2 * ROWS : 3 * ROWS, head_cols(head)] = dq.astype(BF16)


def unpack_kernel(in_ref, gain_sum_ref, gain_ref, dq_ref, dk_ref, dv_ref, grad_gain_ref):
    grad_gain_ref[...] = gain_sum_ref[...] / gain_ref[...]
    for z in range(ZS):
        cols = slice(z * PAIR, (z + 1) * PAIR)
        dk_ref[:, cols] = in_ref[z, 0:ROWS, :]
        dv_ref[:, cols] = in_ref[z, ROWS : 2 * ROWS, :]
        dq_ref[:, cols] = in_ref[z, 2 * ROWS : 3 * ROWS, :]


def call(kernel, outs, *args, scalars=0, scratch=(), flops=1, space=pltpu.VMEM, limit=VMEM_LIMIT):
    specs = [pl.BlockSpec(memory_space=pltpu.SMEM)] * scalars
    specs += [pl.BlockSpec(memory_space=space)] * (len(args) - scalars)
    return pl.pallas_call(
        kernel,
        out_shape=outs,
        in_specs=specs,
        out_specs=[pl.BlockSpec(memory_space=pltpu.VMEM)] * len(outs),
        scratch_shapes=scratch,
        compiler_params=pltpu.CompilerParams(vmem_limit_bytes=limit),
        cost_estimate=pl.CostEstimate(flops=flops, bytes_accessed=0, transcendentals=0),
    )(*args)


def along_z(array):
    groups = [[y * ZS + z for z in range(ZS)] for y in range(ZS)]
    return lax.all_to_all(array, "seq", 0, 0, axis_index_groups=groups, tiled=True)


def shift_z(array, by):
    pairs = [(y * ZS + z, y * ZS + (z + by) % ZS) for y in range(ZS) for z in range(ZS)]
    return lax.ppermute(array, "seq", pairs)


def add_over(array, axis, low):
    size = lax.axis_size(axis)
    if 2 * low >= size:
        return array
    others = [
        lax.ppermute(array, axis, [(i, i ^ bits) for i in range(size)])
        for bits in (low, 2 * low, 3 * low)
    ]
    return (array + others[0]) + (others[1] + others[2])


def add_pairs(array, axis):
    size = lax.axis_size(axis)
    if size == 1:
        return array
    return array + lax.ppermute(array, axis, [(i, i ^ 1) for i in range(size)])


def shift_y(array, by):
    devices = lax.axis_size("seq")
    pairs = [(i, i + ZS * by) for i in range(devices) if 0 <= i + ZS * by < devices]
    return lax.ppermute(array, "seq", pairs)


def per_device(queries, keys, values, gates, lengths, gain, grad_out):
    rows, width = queries.shape[1:]
    shape = jax.ShapeDtypeStruct
    ends = jnp.cumsum(lengths[0])
    info = jnp.concatenate([jnp.stack([lax.axis_index("seq")]), ends]).astype(jnp.int32)
    pair = shape((ZS, 2 * ROWS, PAIR), BF16)
    pair_sums = shape((ZS, 2 * ROWS, PAIR), F32)
    block = shape((BLOCK, PAIR), F32)
    turned = shape((PAIR, BLOCK), F32)
    sums_scratch = [pltpu.VMEM(pair_sums.shape, F32)]

    (kv,) = call(
        pack_kv_kernel,
        [pair],
        keys[0],
        values[0],
        space=pltpu.HBM,
        limit=62 * 1024 * 1024,
        scratch=[pltpu.SemaphoreType.DMA((2 * ZS,))],
    )
    kv0 = along_z(kv)
    kv2 = shift_y(kv0, 2)
    kv1 = shift_y(kv0, 1)
    (qd,) = call(pack_q_kernel, [pair], queries[0], gates[0], grad_out[0], gain[None])
    qd = along_z(qd)
    (own_sum,) = call(forward_own_kernel, [block], info, qd, kv0, scalars=1)
    attended, stats = call(
        forward_kernel,
        [block, shape((ZS, 4 * ZS, ROWS), F32)],
        info,
        qd,
        kv1,
        kv2,
        own_sum,
        scalars=1,
    )
    stats = along_z(stats)
    to2, grad_att, dq, gain_sum = call(
        backward_far_kernel,
        [pair, shape((ZS, ROWS, PAIR), BF16), turned, shape((2, HEAD), F32)],
        info,
        qd,
        kv2,
        attended,
        stats,
        scalars=1,
        scratch=sums_scratch,
    )
    from2 = shift_y(to2, -2)
    to1, dq = call(
        backward_near_kernel,
        [pair, turned],
        info,
        qd,
        kv1,
        grad_att,
        dq,
        scalars=1,
        scratch=sums_scratch,
    )
    from1 = shift_y(to1, -1)
    gain_sum, to1 = lax.optimization_barrier((gain_sum, to1))
    back = call(
        back_kernel,
        [shape((ROWS + EXTRA, PAIR), BF16)] * ZS,
        info,
        attended,
        gain_sum,
        scalars=1,
    )
    back = list(back)
    back[2] = shift_z(back[2], 2)
    back[1] = shift_z(back[1], 1)
    back[3] = shift_z(back[3], 3)
    dq, dkv = call(
        backward_own_kernel, [turned, pair_sums], info, qd, kv0, grad_att, dq, scalars=1
    )
    (gain_sum,) = call(gain_kernel, [shape((1, width), F32)], info, *back, scalars=1)
    output, grad_gate = call(
        norm_kernel,
        [shape((rows, width), BF16)] * 2,
        info,
        *back,
        gates[0],
        grad_out[0],
        gain[None],
        scalars=1,
    )
    (joined,) = call(join_kernel, [shape((ZS, 3 * ROWS, PAIR), BF16)], dq, dkv, from1, from2)
    gain_sum, joined = lax.optimization_barrier((gain_sum, joined))
    gain_sum = add_pairs(gain_sum, "own")
    gain_sum = add_over(add_over(add_over(gain_sum, "own", 2), "seq", 4), "own", 8)
    grad_q, grad_k, grad_v, grad_gain = call(
        unpack_kernel,
        [shape((rows, width), BF16)] * 3 + [shape((1, width), F32)],
        along_z(joined),
        gain_sum,
        gain[None],
    )
    return (output[None], grad_q[None], grad_k[None], grad_v[None], grad_gate[None], grad_gain[0])


def solution(mesh):
    wide = P("own", "seq", None)
    return jax.shard_map(
        per_device,
        mesh=mesh,
        in_specs=(wide, wide, wide, wide, P("own", None), P(), wide),
        out_specs=(wide, wide, wide, wide, wide, P()),
        check_vma=False,
    )
```

```python
import math

import jax
import jax.numpy as jnp
from jax import lax
from jax.experimental import pallas as pl
from jax.experimental.pallas import tpu as pltpu
from jax.sharding import PartitionSpec as P


H = 8
HEAD = 128
ZS = 4
ROWS = 128
PAIR = 2 * HEAD
TILE = 2 * ROWS
BLOCK = ZS * ROWS
EXTRA = 16
F32 = jnp.float32
BF16 = jnp.bfloat16
VMEM_LIMIT = 48 * 1024 * 1024


def dot(a, b, dims):
    return lax.dot_general(a, b, (dims, ((), ())), preferred_element_type=F32)


def iota(shape, dim):
    return lax.broadcasted_iota(jnp.int32, shape, dim)


def bounds(pos, info):
    start = jnp.zeros_like(pos)
    end = jnp.full_like(pos, 1 << 30)
    for user in range(info.shape[0] - 1):
        edge = info[1 + user]
        start = jnp.where(pos >= edge, jnp.maximum(start, edge), start)
        end = jnp.where(pos < edge, jnp.minimum(end, edge), end)
    return start, end - start


def head_cols(head):
    return slice(head * HEAD, (head + 1) * HEAD)


def tile_rows(ref, tile, first, head, tiles=1):
    block = ref[pl.ds(tile * 2, 2 * tiles), first : first + ROWS, head_cols(head)]
    return block.reshape(tiles * TILE, HEAD)


def eye():
    return iota((ROWS, HEAD), 0) == iota((ROWS, HEAD), 1)


def to_row(column):
    return jnp.sum(jnp.where(eye(), column, 0.0), axis=0, keepdims=True)


def to_column(row):
    return jnp.sum(jnp.where(eye(), row, 0.0), axis=1, keepdims=True)


def pack_kv_kernel(k_ref, v_ref, out_ref, sems):
    copies = []
    for z in range(ZS):
        for part, ref in enumerate((k_ref, v_ref)):
            copies.append(
                pltpu.make_async_copy(
                    ref.at[:, z * PAIR : (z + 1) * PAIR],
                    out_ref.at[z, part * ROWS : (part + 1) * ROWS, :],
                    sems.at[2 * z + part],
                )
            )
    for copy in copies:
        copy.start()
    for copy in copies:
        copy.wait()


def pack_q_kernel(q_ref, gates_ref, grad_ref, gain_ref, out_ref):
    for z in range(ZS):
        cols = slice(z * PAIR, (z + 1) * PAIR)
        out_ref[z, 0:ROWS, :] = q_ref[:, cols]
        dnorm = grad_ref[:, cols].astype(F32) * gates_ref[:, cols].astype(F32) * gain_ref[:, cols]
        out_ref[z, ROWS : 2 * ROWS, :] = dnorm.astype(BF16)


def over_keys(info, tile, back, step, total):
    if back == 0:
        return step(0, tile + 1, total)
    block = info[0] // ZS
    first, _ = bounds(block * BLOCK + tile * TILE, info)
    low = jnp.clip(first // TILE - 2 * (block - back), 0, 2)
    return lax.switch(
        low, [lambda t: step(0, 2, t), lambda t: step(1, 1, t), lambda t: t], total
    )


def forward_tiles(info, tile, backs, qd_ref, kv_refs, total):
    scale = 0.5 / math.sqrt(HEAD)
    block = info[0] // ZS
    q = [tile_rows(qd_ref, tile, 0, head) for head in range(2)]
    pos = block * BLOCK + tile * TILE + iota((TILE, 1), 0)
    start, _ = bounds(pos, info)
    for back, kv_ref in zip(backs, kv_refs):

        def step(key_tile, tiles, total, back=back, kv_ref=kv_ref):
            base = (block - back) * BLOCK + key_tile * TILE
            where = iota((1, tiles * TILE), 1)
            allowed = where >= start - base
            if back == 0:
                allowed = allowed & (where <= pos - base)
            sums = []
            for head in range(2):
                k = tile_rows(kv_ref, key_tile, 0, head, tiles)
                v = tile_rows(kv_ref, key_tile, ROWS, head, tiles)
                half_score = dot(q[head], k, ((1,), (1,))) * scale
                silu = half_score + half_score * jnp.tanh(half_score)
                probs = jnp.where(allowed, silu, 0.0).astype(BF16)
                sums.append(total[head] + dot(probs, v, ((1,), (0,))))
            return tuple(sums)

        total = over_keys(info, tile, back, step, total)
    return total


def forward_own_kernel(info, qd_ref, kv0_ref, sum_ref):
    for tile in range(2):
        total = (jnp.zeros((TILE, HEAD), F32),) * 2
        total = forward_tiles(info, tile, (0,), qd_ref, (kv0_ref,), total)
        for head in range(2):
            sum_ref[tile * TILE : (tile + 1) * TILE, head_cols(head)] = total[head]


def forward_kernel(info, qd_ref, kv1_ref, kv2_ref, sum_ref, att_ref, stats_ref):
    block = info[0] // ZS
    for tile in range(2):
        total = tuple(
            sum_ref[tile * TILE : (tile + 1) * TILE, head_cols(head)] for head in range(2)
        )
        total = forward_tiles(info, tile, (1, 2), qd_ref, (kv1_ref, kv2_ref), total)
        _, length = bounds(block * BLOCK + tile * TILE + iota((TILE, 1), 0), info)
        inverse = 1.0 / length.astype(F32)
        attended = [part * inverse for part in total]
        dnorm = [tile_rows(qd_ref, tile, ROWS, head).astype(F32) for head in range(2)]
        mean = jnp.sum(attended[0] + attended[1], axis=1, keepdims=True) / PAIR
        center = [part - mean for part in attended]
        square = jnp.sum(center[0] * center[0] + center[1] * center[1], axis=1, keepdims=True)
        plain = jnp.sum(dnorm[0] + dnorm[1], axis=1, keepdims=True)
        mixed = jnp.sum(dnorm[0] * center[0] + dnorm[1] * center[1], axis=1, keepdims=True)
        for part in range(2):
            span = slice(part * ROWS, (part + 1) * ROWS)
            slot = tile * 2 + part
            for index, column in enumerate((mean, square, plain, mixed)):
                row = to_row(column[span])
                for z in range(ZS):
                    stats_ref[z, index * ZS + slot : index * ZS + slot + 1, :] = row
        for head in range(2):
            att_ref[tile * TILE : (tile + 1) * TILE, head_cols(head)] = attended[head]


def part_cols(info, by, head):
    z = (info[0] - by) % ZS
    return pl.ds(pl.multiple_of(z * PAIR + head * HEAD, HEAD), HEAD)


def norm_kernel(info, in0_ref, in1_ref, in2_ref, in3_ref, *refs):
    gates_ref, grad_ref, gain_ref, out_ref, gate_grad_ref = refs
    width = H * HEAD
    heads = [(by, ref, head) for by, ref in enumerate((in0_ref, in1_ref, in2_ref, in3_ref)) for head in range(2)]
    attended = []
    for by, ref, head in heads:
        mean = to_column(ref[ROWS : ROWS + 1, head_cols(head)].astype(F32))
        attended.append(ref[0:ROWS, head_cols(head)].astype(F32) + mean)
    mean = jnp.sum(sum(attended), axis=1, keepdims=True) / width
    center = [block - mean for block in attended]
    var = jnp.sum(sum(block * block for block in center), axis=1, keepdims=True) / width
    rstd = lax.rsqrt(var + 1e-05)
    for (by, ref, head), block in zip(heads, center):
        cols = part_cols(info, by, head)
        scaled = block * rstd * gain_ref[0:1, cols]
        out_ref[:, cols] = (scaled * gates_ref[:, cols].astype(F32)).astype(BF16)
        gate_grad_ref[:, cols] = (scaled * grad_ref[:, cols].astype(F32)).astype(BF16)


def gain_kernel(info, in0_ref, in1_ref, in2_ref, in3_ref, sum_ref):
    for by, ref in enumerate((in0_ref, in1_ref, in2_ref, in3_ref)):
        for head in range(2):
            three = ref[ROWS : ROWS + EXTRA, head_cols(head)].astype(F32)
            sum_ref[0:1, part_cols(info, by, head)] = three[1:2] + three[2:3] + three[3:4]


def make_grad_att(info, qd_ref, att_ref, stats_ref, grad_ref, gain_ref):
    width = H * HEAD
    block = info[0] // ZS
    sums = [jnp.zeros((1, HEAD), F32) for _ in range(2)]
    for slot in range(ZS):
        stat = [
            [stats_ref[z, index * ZS + slot : index * ZS + slot + 1, :] for z in range(ZS)]
            for index in range(4)
        ]
        means, squares, plains, mixeds = stat
        mean = sum(means) / ZS
        var = (sum(squares) + PAIR * sum((m - mean) * (m - mean) for m in means)) / width
        rstd = lax.rsqrt(var + 1e-05)
        first = sum(plains) / width
        second = rstd * sum(x + (m - mean) * p for x, m, p in zip(mixeds, means, plains)) / width
        _, length = bounds(block * BLOCK + slot * ROWS + iota((1, ROWS), 1), info)
        factor = rstd * (1.0 / length.astype(F32))
        mean, rstd, first, second, factor = (
            to_column(row) for row in (mean, rstd, first, second, factor)
        )
        rows = slice(slot * ROWS, (slot + 1) * ROWS)
        for head in range(2):
            normed = (att_ref[rows, head_cols(head)] - mean) * rstd
            dnorm = qd_ref[slot, ROWS : 2 * ROWS, head_cols(head)].astype(F32)
            sums[head] = sums[head] + jnp.sum(dnorm * normed, axis=0, keepdims=True)
            grad_att = factor * (dnorm - first - normed * second)
            grad_ref[slot, :, head_cols(head)] = grad_att.astype(BF16)
    for head in range(2):
        gain_ref[head : head + 1, :] = sums[head]


def back_kernel(info, att_ref, gain_ref, *back_refs):
    index = iota((EXTRA, HEAD), 0)
    for head in range(2):
        cols = head_cols(head)
        gain = gain_ref[head : head + 1, :]
        high = gain.astype(BF16).astype(F32)
        mid = (gain - high).astype(BF16).astype(F32)
        low = gain - high - mid
        three = jnp.where(index == 1, high, jnp.where(index == 2, mid, low))
        for by, back_ref in enumerate(back_refs):
            slot = (info[0] + by) % ZS
            attended = att_ref[pl.ds(pl.multiple_of(slot * ROWS, ROWS), ROWS), cols]
            middle = jnp.mean(attended, axis=1, keepdims=True).astype(BF16).astype(F32)
            back_ref[0:ROWS, cols] = (attended - middle).astype(BF16)
            extra = jnp.where(index == 0, to_row(middle), three)
            back_ref[ROWS : ROWS + EXTRA, cols] = extra.astype(BF16)


def backward_tiles(info, back, q_ref, kv_ref, grad_ref, dq_ref, dkv_ref):
    scale = 0.5 / math.sqrt(HEAD)
    block = info[0] // ZS
    dkv_ref[...] = jnp.zeros_like(dkv_ref)
    for tile in range(2):
        q = [tile_rows(q_ref, tile, 0, head) for head in range(2)]
        grad = [tile_rows(grad_ref, tile, 0, head) for head in range(2)]
        pos = block * BLOCK + tile * TILE + iota((1, TILE), 1)
        start, _ = bounds(pos, info)
        here = slice(tile * TILE, (tile + 1) * TILE)

        def step(key_tile, tiles, total):
            base = (block - back) * BLOCK + key_tile * TILE
            where = iota((tiles * TILE, 1), 0)
            allowed = where >= start - base
            if back == 0:
                allowed = allowed & (where <= pos - base)
            sums = []
            for head in range(2):
                k = tile_rows(kv_ref, key_tile, 0, head, tiles)
                v = tile_rows(kv_ref, key_tile, ROWS, head, tiles)
                half_score = dot(k, q[head], ((1,), (1,))) * scale
                grad_probs = dot(v, grad[head], ((1,), (1,)))
                tanh = jnp.tanh(half_score)
                twice = 1.0 + tanh
                probs = jnp.where(allowed, half_score * twice, 0.0).astype(BF16)
                slope = twice * (1.0 + half_score * (1.0 - tanh))
                grad_scores = jnp.where(allowed, grad_probs * slope, 0.0).astype(BF16)
                slots = pl.ds(key_tile * 2, 2 * tiles)
                dk = dot(grad_scores, q[head], ((1,), (0,))).reshape(2 * tiles, ROWS, HEAD)
                dv = dot(probs, grad[head], ((1,), (0,))).reshape(2 * tiles, ROWS, HEAD)
                dkv_ref[slots, 0:ROWS, head_cols(head)] += dk
                dkv_ref[slots, ROWS : 2 * ROWS, head_cols(head)] += dv
                sums.append(total[head] + dot(k, grad_scores, ((0,), (0,))))
            return tuple(sums)

        total = tuple(dq_ref[head_cols(head), here] for head in range(2))
        total = over_keys(info, tile, back, step, total)
        for head in range(2):
            dq_ref[head_cols(head), here] = total[head]


def send_sums(dkv_ref, send_ref):
    scale = 0.5 / math.sqrt(HEAD)
    for slot in range(ZS):
        send_ref[slot, 0:ROWS, :] = (dkv_ref[slot, 0:ROWS, :] * scale).astype(BF16)
        send_ref[slot, ROWS : 2 * ROWS, :] = dkv_ref[slot, ROWS : 2 * ROWS, :].astype(BF16)


def backward_far_kernel(
    info, qd_ref, kv2_ref, att_ref, stats_ref, send_ref, grad_ref, dq_ref, gain_ref, dkv_ref
):
    make_grad_att(info, qd_ref, att_ref, stats_ref, grad_ref, gain_ref)
    dq_ref[...] = jnp.zeros_like(dq_ref)
    backward_tiles(info, 2, qd_ref, kv2_ref, grad_ref, dq_ref, dkv_ref)
    send_sums(dkv_ref, send_ref)


def backward_near_kernel(info, qd_ref, kv1_ref, grad_ref, dq_in_ref, send_ref, dq_ref, dkv_ref):
    dq_ref[...] = dq_in_ref[...]
    backward_tiles(info, 1, qd_ref, kv1_ref, grad_ref, dq_ref, dkv_ref)
    send_sums(dkv_ref, send_ref)


def backward_own_kernel(info, qd_ref, kv0_ref, grad_ref, dq_in_ref, dq_ref, dkv_ref):
    dq_ref[...] = dq_in_ref[...]
    backward_tiles(info, 0, qd_ref, kv0_ref, grad_ref, dq_ref, dkv_ref)


def join_kernel(dq_ref, dkv_ref, other1_ref, other2_ref, out_ref):
    scale = 0.5 / math.sqrt(HEAD)
    for slot in range(ZS):
        others = other1_ref[slot].astype(F32) + other2_ref[slot].astype(F32)
        dk = dkv_ref[slot, 0:ROWS, :] * scale + others[0:ROWS]
        dv = dkv_ref[slot, ROWS : 2 * ROWS, :] + others[ROWS : 2 * ROWS]
        out_ref[slot, 0:ROWS, :] = dk.astype(BF16)
        out_ref[slot, ROWS : 2 * ROWS, :] = dv.astype(BF16)
        for head in range(2):
            dq = dq_ref[head_cols(head), slot * ROWS : (slot + 1) * ROWS].T * scale
            out_ref[slot, 2 * ROWS : 3 * ROWS, head_cols(head)] = dq.astype(BF16)


def unpack_kernel(in_ref, gain_sum_ref, gain_ref, dq_ref, dk_ref, dv_ref, grad_gain_ref):
    grad_gain_ref[...] = gain_sum_ref[...] / gain_ref[...]
    for z in range(ZS):
        cols = slice(z * PAIR, (z + 1) * PAIR)
        dk_ref[:, cols] = in_ref[z, 0:ROWS, :]
        dv_ref[:, cols] = in_ref[z, ROWS : 2 * ROWS, :]
        dq_ref[:, cols] = in_ref[z, 2 * ROWS : 3 * ROWS, :]


def call(kernel, outs, *args, scalars=0, scratch=(), flops=1, space=pltpu.VMEM, limit=VMEM_LIMIT):
    specs = [pl.BlockSpec(memory_space=pltpu.SMEM)] * scalars
    specs += [pl.BlockSpec(memory_space=space)] * (len(args) - scalars)
    return pl.pallas_call(
        kernel,
        out_shape=outs,
        in_specs=specs,
        out_specs=[pl.BlockSpec(memory_space=pltpu.VMEM)] * len(outs),
        scratch_shapes=scratch,
        compiler_params=pltpu.CompilerParams(vmem_limit_bytes=limit),
        cost_estimate=pl.CostEstimate(flops=flops, bytes_accessed=0, transcendentals=0),
    )(*args)


def along_z(array):
    groups = [[y * ZS + z for z in range(ZS)] for y in range(ZS)]
    return lax.all_to_all(array, "seq", 0, 0, axis_index_groups=groups, tiled=True)


def shift_z(array, by):
    pairs = [(y * ZS + z, y * ZS + (z + by) % ZS) for y in range(ZS) for z in range(ZS)]
    return lax.ppermute(array, "seq", pairs)


def add_over(array, axis, low):
    size = lax.axis_size(axis)
    if 2 * low >= size:
        return array
    others = [
        lax.ppermute(array, axis, [(i, i ^ bits) for i in range(size)])
        for bits in (low, 2 * low, 3 * low)
    ]
    return (array + others[0]) + (others[1] + others[2])


def add_bits(array, axis, bits):
    size = lax.axis_size(axis)
    for bit in bits:
        if bit < size:
            array = array + lax.ppermute(array, axis, [(i, i ^ bit) for i in range(size)])
    return array


def add_pairs(array, axis):
    size = lax.axis_size(axis)
    if size == 1:
        return array
    return array + lax.ppermute(array, axis, [(i, i ^ 1) for i in range(size)])


def shift_y(array, by):
    devices = lax.axis_size("seq")
    pairs = [(i, i + ZS * by) for i in range(devices) if 0 <= i + ZS * by < devices]
    return lax.ppermute(array, "seq", pairs)


def per_device(queries, keys, values, gates, lengths, gain, grad_out):
    rows, width = queries.shape[1:]
    shape = jax.ShapeDtypeStruct
    ends = jnp.cumsum(lengths[0])
    info = jnp.concatenate([jnp.stack([lax.axis_index("seq")]), ends]).astype(jnp.int32)
    pair = shape((ZS, 2 * ROWS, PAIR), BF16)
    pair_sums = shape((ZS, 2 * ROWS, PAIR), F32)
    block = shape((BLOCK, PAIR), F32)
    turned = shape((PAIR, BLOCK), F32)
    sums_scratch = [pltpu.VMEM(pair_sums.shape, F32)]

    (kv,) = call(
        pack_kv_kernel,
        [pair],
        keys[0],
        values[0],
        space=pltpu.HBM,
        limit=62 * 1024 * 1024,
        scratch=[pltpu.SemaphoreType.DMA((2 * ZS,))],
    )
    kv0 = along_z(kv)
    kv2 = shift_y(kv0, 2)
    kv1 = shift_y(kv0, 1)
    (qd,) = call(pack_q_kernel, [pair], queries[0], gates[0], grad_out[0], gain[None])
    qd = along_z(qd)
    (own_sum,) = call(forward_own_kernel, [block], info, qd, kv0, scalars=1)
    attended, stats = call(
        forward_kernel,
        [block, shape((ZS, 4 * ZS, ROWS), F32)],
        info,
        qd,
        kv1,
        kv2,
        own_sum,
        scalars=1,
    )
    stats = along_z(stats)
    to2, grad_att, dq, gain_sum = call(
        backward_far_kernel,
        [pair, shape((ZS, ROWS, PAIR), BF16), turned, shape((2, HEAD), F32)],
        info,
        qd,
        kv2,
        attended,
        stats,
        scalars=1,
        scratch=sums_scratch,
    )
    from2 = shift_y(to2, -2)
    to1, dq = call(
        backward_near_kernel,
        [pair, turned],
        info,
        qd,
        kv1,
        grad_att,
        dq,
        scalars=1,
        scratch=sums_scratch,
    )
    from1 = shift_y(to1, -1)
    gain_sum, to1 = lax.optimization_barrier((gain_sum, to1))
    back = call(
        back_kernel,
        [shape((ROWS + EXTRA, PAIR), BF16)] * ZS,
        info,
        attended,
        gain_sum,
        scalars=1,
    )
    back = list(back)
    back[2] = shift_z(back[2], 2)
    back[1] = shift_z(back[1], 1)
    back[3] = shift_z(back[3], 3)
    dq, dkv = call(
        backward_own_kernel, [turned, pair_sums], info, qd, kv0, grad_att, dq, scalars=1
    )
    (gain_sum,) = call(gain_kernel, [shape((1, width), F32)], info, *back, scalars=1)
    output, grad_gate = call(
        norm_kernel,
        [shape((rows, width), BF16)] * 2,
        info,
        *back,
        gates[0],
        grad_out[0],
        gain[None],
        scalars=1,
    )
    (joined,) = call(join_kernel, [shape((ZS, 3 * ROWS, PAIR), BF16)], dq, dkv, from1, from2)
    gain_sum, joined = lax.optimization_barrier((gain_sum, joined))
    gain_sum = add_pairs(gain_sum, "own")
    gain_sum = add_bits(add_bits(add_bits(gain_sum, "own", (2, 4)), "seq", (4, 8)), "own", (8, 16))
    grad_q, grad_k, grad_v, grad_gain = call(
        unpack_kernel,
        [shape((rows, width), BF16)] * 3 + [shape((1, width), F32)],
        along_z(joined),
        gain_sum,
        gain[None],
    )
    return (output[None], grad_q[None], grad_k[None], grad_v[None], grad_gate[None], grad_gain[0])


def solution(mesh):
    wide = P("own", "seq", None)
    return jax.shard_map(
        per_device,
        mesh=mesh,
        in_specs=(wide, wide, wide, wide, P("own", None), P(), wide),
        out_specs=(wide, wide, wide, wide, wide, P()),
        check_vma=False,
    )
```

```python
import math

import jax
import jax.numpy as jnp
from jax import lax
from jax.experimental import pallas as pl
from jax.experimental.pallas import tpu as pltpu
from jax.sharding import PartitionSpec as P


H = 8
HEAD = 128
ZS = 4
ROWS = 128
PAIR = 2 * HEAD
TILE = 2 * ROWS
BLOCK = ZS * ROWS
EXTRA = 16
F32 = jnp.float32
BF16 = jnp.bfloat16
VMEM_LIMIT = 48 * 1024 * 1024


def dot(a, b, dims):
    return lax.dot_general(a, b, (dims, ((), ())), preferred_element_type=F32)


def iota(shape, dim):
    return lax.broadcasted_iota(jnp.int32, shape, dim)


def bounds(pos, info):
    start = jnp.zeros_like(pos)
    end = jnp.full_like(pos, 1 << 30)
    for user in range(info.shape[0] - 1):
        edge = info[1 + user]
        start = jnp.where(pos >= edge, jnp.maximum(start, edge), start)
        end = jnp.where(pos < edge, jnp.minimum(end, edge), end)
    return start, end - start


def head_cols(head):
    return slice(head * HEAD, (head + 1) * HEAD)


def tile_rows(ref, tile, first, head, tiles=1):
    block = ref[pl.ds(tile * 2, 2 * tiles), first : first + ROWS, head_cols(head)]
    return block.reshape(tiles * TILE, HEAD)


def eye():
    return iota((ROWS, HEAD), 0) == iota((ROWS, HEAD), 1)


def to_row(column):
    return jnp.sum(jnp.where(eye(), column, 0.0), axis=0, keepdims=True)


def to_column(row):
    return jnp.sum(jnp.where(eye(), row, 0.0), axis=1, keepdims=True)


def pack_kv_kernel(k_ref, v_ref, out_ref, sems):
    copies = []
    for z in range(ZS):
        for part, ref in enumerate((k_ref, v_ref)):
            copies.append(
                pltpu.make_async_copy(
                    ref.at[:, z * PAIR : (z + 1) * PAIR],
                    out_ref.at[z, part * ROWS : (part + 1) * ROWS, :],
                    sems.at[2 * z + part],
                )
            )
    for copy in copies:
        copy.start()
    for copy in copies:
        copy.wait()


def pack_q_kernel(q_ref, gates_ref, grad_ref, gain_ref, out_ref):
    for z in range(ZS):
        cols = slice(z * PAIR, (z + 1) * PAIR)
        out_ref[z, 0:ROWS, :] = q_ref[:, cols]
        dnorm = grad_ref[:, cols].astype(F32) * gates_ref[:, cols].astype(F32) * gain_ref[:, cols]
        out_ref[z, ROWS : 2 * ROWS, :] = dnorm.astype(BF16)


def over_keys(info, tile, back, step, total):
    if back == 0:
        return step(0, tile + 1, total)
    block = info[0] // ZS
    first, _ = bounds(block * BLOCK + tile * TILE, info)
    low = jnp.clip(first // TILE - 2 * (block - back), 0, 2)
    return lax.switch(
        low, [lambda t: step(0, 2, t), lambda t: step(1, 1, t), lambda t: t], total
    )


def forward_tiles(info, tile, backs, qd_ref, kv_refs, total):
    scale = 0.5 / math.sqrt(HEAD)
    block = info[0] // ZS
    q = [tile_rows(qd_ref, tile, 0, head) for head in range(2)]
    pos = block * BLOCK + tile * TILE + iota((TILE, 1), 0)
    start, _ = bounds(pos, info)
    for back, kv_ref in zip(backs, kv_refs):

        def step(key_tile, tiles, total, back=back, kv_ref=kv_ref):
            base = (block - back) * BLOCK + key_tile * TILE
            where = iota((1, tiles * TILE), 1)
            allowed = where >= start - base
            if back == 0:
                allowed = allowed & (where <= pos - base)
            sums = []
            for head in range(2):
                k = tile_rows(kv_ref, key_tile, 0, head, tiles)
                v = tile_rows(kv_ref, key_tile, ROWS, head, tiles)
                half_score = dot(q[head], k, ((1,), (1,))) * scale
                silu = half_score + half_score * jnp.tanh(half_score)
                probs = jnp.where(allowed, silu, 0.0).astype(BF16)
                sums.append(total[head] + dot(probs, v, ((1,), (0,))))
            return tuple(sums)

        total = over_keys(info, tile, back, step, total)
    return total


def forward_own_kernel(info, qd_ref, kv0_ref, sum_ref):
    for tile in range(2):
        total = (jnp.zeros((TILE, HEAD), F32),) * 2
        total = forward_tiles(info, tile, (0,), qd_ref, (kv0_ref,), total)
        for head in range(2):
            sum_ref[tile * TILE : (tile + 1) * TILE, head_cols(head)] = total[head]


def forward_kernel(info, qd_ref, kv1_ref, kv2_ref, sum_ref, att_ref, stats_ref):
    block = info[0] // ZS
    for tile in range(2):
        total = tuple(
            sum_ref[tile * TILE : (tile + 1) * TILE, head_cols(head)] for head in range(2)
        )
        total = forward_tiles(info, tile, (1, 2), qd_ref, (kv1_ref, kv2_ref), total)
        _, length = bounds(block * BLOCK + tile * TILE + iota((TILE, 1), 0), info)
        inverse = 1.0 / length.astype(F32)
        attended = [part * inverse for part in total]
        dnorm = [tile_rows(qd_ref, tile, ROWS, head).astype(F32) for head in range(2)]
        mean = jnp.sum(attended[0] + attended[1], axis=1, keepdims=True) / PAIR
        center = [part - mean for part in attended]
        square = jnp.sum(center[0] * center[0] + center[1] * center[1], axis=1, keepdims=True)
        plain = jnp.sum(dnorm[0] + dnorm[1], axis=1, keepdims=True)
        mixed = jnp.sum(dnorm[0] * center[0] + dnorm[1] * center[1], axis=1, keepdims=True)
        for part in range(2):
            span = slice(part * ROWS, (part + 1) * ROWS)
            slot = tile * 2 + part
            for index, column in enumerate((mean, square, plain, mixed)):
                row = to_row(column[span])
                for z in range(ZS):
                    stats_ref[z, index * ZS + slot : index * ZS + slot + 1, :] = row
        for head in range(2):
            att_ref[tile * TILE : (tile + 1) * TILE, head_cols(head)] = attended[head]


def part_cols(info, by, head):
    z = (info[0] - by) % ZS
    return pl.ds(pl.multiple_of(z * PAIR + head * HEAD, HEAD), HEAD)


def norm_kernel(info, in0_ref, in1_ref, in2_ref, in3_ref, *refs):
    gates_ref, grad_ref, gain_ref, out_ref, gate_grad_ref = refs
    width = H * HEAD
    heads = [(by, ref, head) for by, ref in enumerate((in0_ref, in1_ref, in2_ref, in3_ref)) for head in range(2)]
    attended = []
    for by, ref, head in heads:
        extra = ref[ROWS : ROWS + EXTRA, head_cols(head)].astype(F32)
        mean = to_column(extra[0:1])
        attended.append(ref[0:ROWS, head_cols(head)].astype(F32) + mean)
    mean = jnp.sum(sum(attended), axis=1, keepdims=True) / width
    center = [block - mean for block in attended]
    var = jnp.sum(sum(block * block for block in center), axis=1, keepdims=True) / width
    rstd = lax.rsqrt(var + 1e-05)
    for (by, ref, head), block in zip(heads, center):
        cols = part_cols(info, by, head)
        scaled = block * rstd * gain_ref[0:1, cols]
        out_ref[:, cols] = (scaled * gates_ref[:, cols].astype(F32)).astype(BF16)
        gate_grad_ref[:, cols] = (scaled * grad_ref[:, cols].astype(F32)).astype(BF16)


def gain_kernel(info, in0_ref, in1_ref, in2_ref, in3_ref, sum_ref):
    for by, ref in enumerate((in0_ref, in1_ref, in2_ref, in3_ref)):
        for head in range(2):
            three = ref[ROWS : ROWS + EXTRA, head_cols(head)].astype(F32)
            sum_ref[0:1, part_cols(info, by, head)] = three[1:2] + three[2:3] + three[3:4]


def make_grad_att(info, qd_ref, att_ref, stats_ref, grad_ref, gain_ref):
    width = H * HEAD
    block = info[0] // ZS
    sums = [jnp.zeros((1, HEAD), F32) for _ in range(2)]
    for slot in range(ZS):
        stat = [
            [stats_ref[z, index * ZS + slot : index * ZS + slot + 1, :] for z in range(ZS)]
            for index in range(4)
        ]
        means, squares, plains, mixeds = stat
        mean = sum(means) / ZS
        var = (sum(squares) + PAIR * sum((m - mean) * (m - mean) for m in means)) / width
        rstd = lax.rsqrt(var + 1e-05)
        first = sum(plains) / width
        second = rstd * sum(x + (m - mean) * p for x, m, p in zip(mixeds, means, plains)) / width
        _, length = bounds(block * BLOCK + slot * ROWS + iota((1, ROWS), 1), info)
        factor = rstd * (1.0 / length.astype(F32))
        mean, rstd, first, second, factor = (
            to_column(row) for row in (mean, rstd, first, second, factor)
        )
        rows = slice(slot * ROWS, (slot + 1) * ROWS)
        for head in range(2):
            normed = (att_ref[rows, head_cols(head)] - mean) * rstd
            dnorm = qd_ref[slot, ROWS : 2 * ROWS, head_cols(head)].astype(F32)
            sums[head] = sums[head] + jnp.sum(dnorm * normed, axis=0, keepdims=True)
            grad_att = factor * (dnorm - first - normed * second)
            grad_ref[slot, :, head_cols(head)] = grad_att.astype(BF16)
    for head in range(2):
        gain_ref[head : head + 1, :] = sums[head]


def back_kernel(info, att_ref, gain_ref, *back_refs):
    index = iota((EXTRA, HEAD), 0)
    for head in range(2):
        cols = head_cols(head)
        gain = gain_ref[head : head + 1, :]
        high = gain.astype(BF16).astype(F32)
        mid = (gain - high).astype(BF16).astype(F32)
        low = gain - high - mid
        three = jnp.where(index == 1, high, jnp.where(index == 2, mid, low))
        for by, back_ref in enumerate(back_refs):
            slot = (info[0] + by) % ZS
            attended = att_ref[pl.ds(pl.multiple_of(slot * ROWS, ROWS), ROWS), cols]
            middle = jnp.mean(attended, axis=1, keepdims=True).astype(BF16).astype(F32)
            back_ref[0:ROWS, cols] = (attended - middle).astype(BF16)
            extra = jnp.where(index == 0, to_row(middle), three)
            back_ref[ROWS : ROWS + EXTRA, cols] = extra.astype(BF16)


def backward_tiles(info, back, q_ref, kv_ref, grad_ref, dq_ref, dkv_ref):
    scale = 0.5 / math.sqrt(HEAD)
    block = info[0] // ZS
    dkv_ref[...] = jnp.zeros_like(dkv_ref)
    for tile in range(2):
        q = [tile_rows(q_ref, tile, 0, head) for head in range(2)]
        grad = [tile_rows(grad_ref, tile, 0, head) for head in range(2)]
        pos = block * BLOCK + tile * TILE + iota((1, TILE), 1)
        start, _ = bounds(pos, info)
        here = slice(tile * TILE, (tile + 1) * TILE)

        def step(key_tile, tiles, total):
            base = (block - back) * BLOCK + key_tile * TILE
            where = iota((tiles * TILE, 1), 0)
            allowed = where >= start - base
            if back == 0:
                allowed = allowed & (where <= pos - base)
            sums = []
            for head in range(2):
                k = tile_rows(kv_ref, key_tile, 0, head, tiles)
                v = tile_rows(kv_ref, key_tile, ROWS, head, tiles)
                half_score = dot(k, q[head], ((1,), (1,))) * scale
                grad_probs = dot(v, grad[head], ((1,), (1,)))
                tanh = jnp.tanh(half_score)
                twice = 1.0 + tanh
                probs = jnp.where(allowed, half_score * twice, 0.0).astype(BF16)
                slope = twice * (1.0 + half_score * (1.0 - tanh))
                grad_scores = jnp.where(allowed, grad_probs * slope, 0.0).astype(BF16)
                slots = pl.ds(key_tile * 2, 2 * tiles)
                dk = dot(grad_scores, q[head], ((1,), (0,))).reshape(2 * tiles, ROWS, HEAD)
                dv = dot(probs, grad[head], ((1,), (0,))).reshape(2 * tiles, ROWS, HEAD)
                dkv_ref[slots, 0:ROWS, head_cols(head)] += dk
                dkv_ref[slots, ROWS : 2 * ROWS, head_cols(head)] += dv
                sums.append(total[head] + dot(k, grad_scores, ((0,), (0,))))
            return tuple(sums)

        total = tuple(dq_ref[head_cols(head), here] for head in range(2))
        total = over_keys(info, tile, back, step, total)
        for head in range(2):
            dq_ref[head_cols(head), here] = total[head]


def send_sums(dkv_ref, send_ref):
    scale = 0.5 / math.sqrt(HEAD)
    for slot in range(ZS):
        send_ref[slot, 0:ROWS, :] = (dkv_ref[slot, 0:ROWS, :] * scale).astype(BF16)
        send_ref[slot, ROWS : 2 * ROWS, :] = dkv_ref[slot, ROWS : 2 * ROWS, :].astype(BF16)


def backward_far_kernel(
    info, qd_ref, kv2_ref, att_ref, stats_ref, send_ref, grad_ref, dq_ref, gain_ref, dkv_ref
):
    make_grad_att(info, qd_ref, att_ref, stats_ref, grad_ref, gain_ref)
    dq_ref[...] = jnp.zeros_like(dq_ref)
    backward_tiles(info, 2, qd_ref, kv2_ref, grad_ref, dq_ref, dkv_ref)
    send_sums(dkv_ref, send_ref)


def backward_near_kernel(info, qd_ref, kv1_ref, grad_ref, dq_in_ref, send_ref, dq_ref, dkv_ref):
    dq_ref[...] = dq_in_ref[...]
    backward_tiles(info, 1, qd_ref, kv1_ref, grad_ref, dq_ref, dkv_ref)
    send_sums(dkv_ref, send_ref)


def backward_own_kernel(info, qd_ref, kv0_ref, grad_ref, dq_in_ref, dq_ref, dkv_ref):
    dq_ref[...] = dq_in_ref[...]
    backward_tiles(info, 0, qd_ref, kv0_ref, grad_ref, dq_ref, dkv_ref)


def join_kernel(dq_ref, dkv_ref, other1_ref, other2_ref, out_ref):
    scale = 0.5 / math.sqrt(HEAD)
    for slot in range(ZS):
        others = other1_ref[slot].astype(F32) + other2_ref[slot].astype(F32)
        dk = dkv_ref[slot, 0:ROWS, :] * scale + others[0:ROWS]
        dv = dkv_ref[slot, ROWS : 2 * ROWS, :] + others[ROWS : 2 * ROWS]
        out_ref[slot, 0:ROWS, :] = dk.astype(BF16)
        out_ref[slot, ROWS : 2 * ROWS, :] = dv.astype(BF16)
        for head in range(2):
            dq = dq_ref[head_cols(head), slot * ROWS : (slot + 1) * ROWS].T * scale
            out_ref[slot, 2 * ROWS : 3 * ROWS, head_cols(head)] = dq.astype(BF16)


def unpack_kernel(in_ref, gain_sum_ref, gain_ref, dq_ref, dk_ref, dv_ref, grad_gain_ref):
    grad_gain_ref[...] = gain_sum_ref[...] / gain_ref[...]
    for z in range(ZS):
        cols = slice(z * PAIR, (z + 1) * PAIR)
        dk_ref[:, cols] = in_ref[z, 0:ROWS, :]
        dv_ref[:, cols] = in_ref[z, ROWS : 2 * ROWS, :]
        dq_ref[:, cols] = in_ref[z, 2 * ROWS : 3 * ROWS, :]


def call(kernel, outs, *args, scalars=0, scratch=(), flops=1, space=pltpu.VMEM, limit=VMEM_LIMIT):
    specs = [pl.BlockSpec(memory_space=pltpu.SMEM)] * scalars
    specs += [pl.BlockSpec(memory_space=space)] * (len(args) - scalars)
    return pl.pallas_call(
        kernel,
        out_shape=outs,
        in_specs=specs,
        out_specs=[pl.BlockSpec(memory_space=pltpu.VMEM)] * len(outs),
        scratch_shapes=scratch,
        compiler_params=pltpu.CompilerParams(vmem_limit_bytes=limit),
        cost_estimate=pl.CostEstimate(flops=flops, bytes_accessed=0, transcendentals=0),
    )(*args)


def along_z(array):
    groups = [[y * ZS + z for z in range(ZS)] for y in range(ZS)]
    return lax.all_to_all(array, "seq", 0, 0, axis_index_groups=groups, tiled=True)


def shift_z(array, by):
    pairs = [(y * ZS + z, y * ZS + (z + by) % ZS) for y in range(ZS) for z in range(ZS)]
    return lax.ppermute(array, "seq", pairs)


def add_over(array, axis, low):
    size = lax.axis_size(axis)
    if 2 * low >= size:
        return array
    others = [
        lax.ppermute(array, axis, [(i, i ^ bits) for i in range(size)])
        for bits in (low, 2 * low, 3 * low)
    ]
    return (array + others[0]) + (others[1] + others[2])


def add_bits(array, axis, bits):
    size = lax.axis_size(axis)
    for bit in bits:
        if bit < size:
            array = array + lax.ppermute(array, axis, [(i, i ^ bit) for i in range(size)])
    return array


def add_pairs(array, axis):
    size = lax.axis_size(axis)
    if size == 1:
        return array
    return array + lax.ppermute(array, axis, [(i, i ^ 1) for i in range(size)])


def shift_y(array, by):
    devices = lax.axis_size("seq")
    pairs = [(i, i + ZS * by) for i in range(devices) if 0 <= i + ZS * by < devices]
    return lax.ppermute(array, "seq", pairs)


def per_device(queries, keys, values, gates, lengths, gain, grad_out):
    rows, width = queries.shape[1:]
    shape = jax.ShapeDtypeStruct
    ends = jnp.cumsum(lengths[0])
    info = jnp.concatenate([jnp.stack([lax.axis_index("seq")]), ends]).astype(jnp.int32)
    pair = shape((ZS, 2 * ROWS, PAIR), BF16)
    pair_sums = shape((ZS, 2 * ROWS, PAIR), F32)
    block = shape((BLOCK, PAIR), F32)
    turned = shape((PAIR, BLOCK), F32)
    sums_scratch = [pltpu.VMEM(pair_sums.shape, F32)]

    (kv,) = call(
        pack_kv_kernel,
        [pair],
        keys[0],
        values[0],
        space=pltpu.HBM,
        limit=62 * 1024 * 1024,
        scratch=[pltpu.SemaphoreType.DMA((2 * ZS,))],
    )
    kv0 = along_z(kv)
    kv2 = shift_y(kv0, 2)
    kv1 = shift_y(kv0, 1)
    (qd,) = call(pack_q_kernel, [pair], queries[0], gates[0], grad_out[0], gain[None])
    qd = along_z(qd)
    (own_sum,) = call(forward_own_kernel, [block], info, qd, kv0, scalars=1)
    attended, stats = call(
        forward_kernel,
        [block, shape((ZS, 4 * ZS, ROWS), F32)],
        info,
        qd,
        kv1,
        kv2,
        own_sum,
        scalars=1,
    )
    stats = along_z(stats)
    to2, grad_att, dq, gain_sum = call(
        backward_far_kernel,
        [pair, shape((ZS, ROWS, PAIR), BF16), turned, shape((2, HEAD), F32)],
        info,
        qd,
        kv2,
        attended,
        stats,
        scalars=1,
        scratch=sums_scratch,
    )
    from2 = shift_y(to2, -2)
    to1, dq = call(
        backward_near_kernel,
        [pair, turned],
        info,
        qd,
        kv1,
        grad_att,
        dq,
        scalars=1,
        scratch=sums_scratch,
    )
    from1 = shift_y(to1, -1)
    gain_sum, to1 = lax.optimization_barrier((gain_sum, to1))
    back = call(
        back_kernel,
        [shape((ROWS + EXTRA, PAIR), BF16)] * ZS,
        info,
        attended,
        gain_sum,
        scalars=1,
    )
    back = list(back)
    back[2] = shift_z(back[2], 2)
    back[1] = shift_z(back[1], 1)
    back[3] = shift_z(back[3], 3)
    dq, dkv = call(
        backward_own_kernel, [turned, pair_sums], info, qd, kv0, grad_att, dq, scalars=1
    )
    (gain_sum,) = call(gain_kernel, [shape((1, width), F32)], info, *back, scalars=1)
    output, grad_gate = call(
        norm_kernel,
        [shape((rows, width), BF16)] * 2,
        info,
        *back,
        gates[0],
        grad_out[0],
        gain[None],
        scalars=1,
    )
    (joined,) = call(join_kernel, [shape((ZS, 3 * ROWS, PAIR), BF16)], dq, dkv, from1, from2)
    gain_sum, joined = lax.optimization_barrier((gain_sum, joined))
    gain_sum = add_pairs(gain_sum, "own")
    gain_sum = add_bits(add_bits(add_bits(gain_sum, "own", (2, 4)), "seq", (4, 8)), "own", (8, 16))
    grad_q, grad_k, grad_v, grad_gain = call(
        unpack_kernel,
        [shape((rows, width), BF16)] * 3 + [shape((1, width), F32)],
        along_z(joined),
        gain_sum,
        gain[None],
    )
    return (output[None], grad_q[None], grad_k[None], grad_v[None], grad_gate[None], grad_gain[0])


def solution(mesh):
    wide = P("own", "seq", None)
    return jax.shard_map(
        per_device,
        mesh=mesh,
        in_specs=(wide, wide, wide, wide, P("own", None), P(), wide),
        out_specs=(wide, wide, wide, wide, wide, P()),
        check_vma=False,
    )
```

```python
import math

import jax
import jax.numpy as jnp
from jax import lax
from jax.experimental import pallas as pl
from jax.experimental.pallas import tpu as pltpu
from jax.sharding import PartitionSpec as P


H = 8
HEAD = 128
ZS = 4
ROWS = 128
PAIR = 2 * HEAD
TILE = 2 * ROWS
BLOCK = ZS * ROWS
EXTRA = 16
F32 = jnp.float32
BF16 = jnp.bfloat16
VMEM_LIMIT = 48 * 1024 * 1024


def dot(a, b, dims):
    return lax.dot_general(a, b, (dims, ((), ())), preferred_element_type=F32)


def iota(shape, dim):
    return lax.broadcasted_iota(jnp.int32, shape, dim)


def bounds(pos, info):
    start = jnp.zeros_like(pos)
    end = jnp.full_like(pos, 1 << 30)
    for user in range(info.shape[0] - 1):
        edge = info[1 + user]
        start = jnp.where(pos >= edge, jnp.maximum(start, edge), start)
        end = jnp.where(pos < edge, jnp.minimum(end, edge), end)
    return start, end - start


def head_cols(head):
    return slice(head * HEAD, (head + 1) * HEAD)


def tile_rows(ref, tile, first, head, tiles=1):
    block = ref[pl.ds(tile * 2, 2 * tiles), first : first + ROWS, head_cols(head)]
    return block.reshape(tiles * TILE, HEAD)


def eye():
    return iota((ROWS, HEAD), 0) == iota((ROWS, HEAD), 1)


def to_row(column):
    return jnp.sum(jnp.where(eye(), column, 0.0), axis=0, keepdims=True)


def to_column(row):
    return jnp.sum(jnp.where(eye(), row, 0.0), axis=1, keepdims=True)


def pack_kv_kernel(k_ref, v_ref, out_ref, sems):
    copies = []
    for z in range(ZS):
        for part, ref in enumerate((k_ref, v_ref)):
            copies.append(
                pltpu.make_async_copy(
                    ref.at[:, z * PAIR : (z + 1) * PAIR],
                    out_ref.at[z, part * ROWS : (part + 1) * ROWS, :],
                    sems.at[2 * z + part],
                )
            )
    for copy in copies:
        copy.start()
    for copy in copies:
        copy.wait()


def pack_q_kernel(q_ref, gates_ref, grad_ref, gain_ref, out_ref):
    for z in range(ZS):
        cols = slice(z * PAIR, (z + 1) * PAIR)
        out_ref[z, 0:ROWS, :] = q_ref[:, cols]
        dnorm = grad_ref[:, cols].astype(F32) * gates_ref[:, cols].astype(F32) * gain_ref[:, cols]
        out_ref[z, ROWS : 2 * ROWS, :] = dnorm.astype(BF16)


def over_keys(info, tile, back, step, total):
    if back == 0:
        return step(0, tile + 1, total)
    block = info[0] // ZS
    first, _ = bounds(block * BLOCK + tile * TILE, info)
    low = jnp.clip(first // TILE - 2 * (block - back), 0, 2)
    return lax.switch(
        low, [lambda t: step(0, 2, t), lambda t: step(1, 1, t), lambda t: t], total
    )


def forward_tiles(info, tile, backs, qd_ref, kv_refs, total):
    scale = 0.5 / math.sqrt(HEAD)
    block = info[0] // ZS
    q = [tile_rows(qd_ref, tile, 0, head) for head in range(2)]
    pos = block * BLOCK + tile * TILE + iota((TILE, 1), 0)
    start, _ = bounds(pos, info)
    for back, kv_ref in zip(backs, kv_refs):

        def step(key_tile, tiles, total, back=back, kv_ref=kv_ref):
            base = (block - back) * BLOCK + key_tile * TILE
            where = iota((1, tiles * TILE), 1)
            allowed = where >= start - base
            if back == 0:
                allowed = allowed & (where <= pos - base)
            sums = []
            for head in range(2):
                k = tile_rows(kv_ref, key_tile, 0, head, tiles)
                v = tile_rows(kv_ref, key_tile, ROWS, head, tiles)
                half_score = dot(q[head], k, ((1,), (1,))) * scale
                silu = half_score + half_score * jnp.tanh(half_score)
                probs = jnp.where(allowed, silu, 0.0).astype(BF16)
                sums.append(total[head] + dot(probs, v, ((1,), (0,))))
            return tuple(sums)

        total = over_keys(info, tile, back, step, total)
    return total


def forward_own_kernel(info, qd_ref, kv0_ref, sum_ref):
    for tile in range(2):
        total = (jnp.zeros((TILE, HEAD), F32),) * 2
        total = forward_tiles(info, tile, (0,), qd_ref, (kv0_ref,), total)
        for head in range(2):
            sum_ref[tile * TILE : (tile + 1) * TILE, head_cols(head)] = total[head]


def forward_kernel(info, qd_ref, kv1_ref, kv2_ref, sum_ref, att_ref, stats_ref):
    block = info[0] // ZS
    for tile in range(2):
        total = tuple(
            sum_ref[tile * TILE : (tile + 1) * TILE, head_cols(head)] for head in range(2)
        )
        total = forward_tiles(info, tile, (1, 2), qd_ref, (kv1_ref, kv2_ref), total)
        _, length = bounds(block * BLOCK + tile * TILE + iota((TILE, 1), 0), info)
        inverse = 1.0 / length.astype(F32)
        attended = [part * inverse for part in total]
        dnorm = [tile_rows(qd_ref, tile, ROWS, head).astype(F32) for head in range(2)]
        mean = jnp.sum(attended[0] + attended[1], axis=1, keepdims=True) / PAIR
        center = [part - mean for part in attended]
        square = jnp.sum(center[0] * center[0] + center[1] * center[1], axis=1, keepdims=True)
        plain = jnp.sum(dnorm[0] + dnorm[1], axis=1, keepdims=True)
        mixed = jnp.sum(dnorm[0] * center[0] + dnorm[1] * center[1], axis=1, keepdims=True)
        for part in range(2):
            span = slice(part * ROWS, (part + 1) * ROWS)
            slot = tile * 2 + part
            for index, column in enumerate((mean, square, plain, mixed)):
                row = to_row(column[span])
                for z in range(ZS):
                    stats_ref[z, index * ZS + slot : index * ZS + slot + 1, :] = row
        for head in range(2):
            att_ref[tile * TILE : (tile + 1) * TILE, head_cols(head)] = attended[head]


def part_cols(info, by, head):
    z = (info[0] - by) % ZS
    return pl.ds(pl.multiple_of(z * PAIR + head * HEAD, HEAD), HEAD)


def norm_kernel(info, in0_ref, in1_ref, in2_ref, in3_ref, *refs):
    gates_ref, grad_ref, gain_ref, out_ref, gate_grad_ref = refs
    width = H * HEAD
    heads = [(by, ref, head) for by, ref in enumerate((in0_ref, in1_ref, in2_ref, in3_ref)) for head in range(2)]
    attended = []
    for by, ref, head in heads:
        extra = ref[ROWS : ROWS + EXTRA, head_cols(head)].astype(F32)
        mean = to_column(extra[0:1])
        attended.append(ref[0:ROWS, head_cols(head)].astype(F32) + mean)
    mean = jnp.sum(sum(attended), axis=1, keepdims=True) / width
    center = [block - mean for block in attended]
    var = jnp.sum(sum(block * block for block in center), axis=1, keepdims=True) / width
    rstd = lax.rsqrt(var + 1e-05)
    for (by, ref, head), block in zip(heads, center):
        cols = part_cols(info, by, head)
        scaled = block * rstd * gain_ref[0:1, cols]
        out_ref[:, cols] = (scaled * gates_ref[:, cols].astype(F32)).astype(BF16)
        gate_grad_ref[:, cols] = (scaled * grad_ref[:, cols].astype(F32)).astype(BF16)


def gain_kernel(info, in0_ref, in1_ref, in2_ref, in3_ref, sum_ref):
    for by, ref in enumerate((in0_ref, in1_ref, in2_ref, in3_ref)):
        for head in range(2):
            three = ref[ROWS : ROWS + EXTRA, head_cols(head)].astype(F32)
            sum_ref[0:1, part_cols(info, by, head)] = three[1:2] + three[2:3] + three[3:4]


def make_grad_att(info, qd_ref, att_ref, stats_ref, grad_ref, gain_ref):
    width = H * HEAD
    block = info[0] // ZS
    sums = [jnp.zeros((1, HEAD), F32) for _ in range(2)]
    for slot in range(ZS):
        stat = [
            [stats_ref[z, index * ZS + slot : index * ZS + slot + 1, :] for z in range(ZS)]
            for index in range(4)
        ]
        means, squares, plains, mixeds = stat
        mean = sum(means) / ZS
        var = (sum(squares) + PAIR * sum((m - mean) * (m - mean) for m in means)) / width
        rstd = lax.rsqrt(var + 1e-05)
        first = sum(plains) / width
        second = rstd * sum(x + (m - mean) * p for x, m, p in zip(mixeds, means, plains)) / width
        _, length = bounds(block * BLOCK + slot * ROWS + iota((1, ROWS), 1), info)
        factor = rstd * (1.0 / length.astype(F32))
        mean, rstd, first, second, factor = (
            to_column(row) for row in (mean, rstd, first, second, factor)
        )
        rows = slice(slot * ROWS, (slot + 1) * ROWS)
        for head in range(2):
            normed = (att_ref[rows, head_cols(head)] - mean) * rstd
            dnorm = qd_ref[slot, ROWS : 2 * ROWS, head_cols(head)].astype(F32)
            sums[head] = sums[head] + jnp.sum(dnorm * normed, axis=0, keepdims=True)
            grad_att = factor * (dnorm - first - normed * second)
            grad_ref[slot, :, head_cols(head)] = grad_att.astype(BF16)
    for head in range(2):
        gain_ref[head : head + 1, :] = sums[head]


def back_kernel(info, att_ref, gain_ref, *back_refs):
    index = iota((EXTRA, HEAD), 0)
    for head in range(2):
        cols = head_cols(head)
        gain = gain_ref[head : head + 1, :]
        high = gain.astype(BF16).astype(F32)
        mid = (gain - high).astype(BF16).astype(F32)
        low = gain - high - mid
        three = jnp.where(index == 1, high, jnp.where(index == 2, mid, low))
        for by, back_ref in enumerate(back_refs):
            slot = (info[0] + by) % ZS
            attended = att_ref[pl.ds(pl.multiple_of(slot * ROWS, ROWS), ROWS), cols]
            middle = jnp.mean(attended, axis=1, keepdims=True).astype(BF16).astype(F32)
            back_ref[0:ROWS, cols] = (attended - middle).astype(BF16)
            extra = jnp.where(index == 0, to_row(middle), three)
            back_ref[ROWS : ROWS + EXTRA, cols] = extra.astype(BF16)


def backward_tiles(info, back, q_ref, kv_ref, grad_ref, dq_ref, dkv_ref):
    scale = 0.5 / math.sqrt(HEAD)
    block = info[0] // ZS
    dkv_ref[...] = jnp.zeros_like(dkv_ref)
    for tile in range(2):
        q = [tile_rows(q_ref, tile, 0, head) for head in range(2)]
        grad = [tile_rows(grad_ref, tile, 0, head) for head in range(2)]
        pos = block * BLOCK + tile * TILE + iota((1, TILE), 1)
        start, _ = bounds(pos, info)
        here = slice(tile * TILE, (tile + 1) * TILE)

        def step(key_tile, tiles, total):
            base = (block - back) * BLOCK + key_tile * TILE
            where = iota((tiles * TILE, 1), 0)
            allowed = where >= start - base
            if back == 0:
                allowed = allowed & (where <= pos - base)
            sums = []
            for head in range(2):
                k = tile_rows(kv_ref, key_tile, 0, head, tiles)
                v = tile_rows(kv_ref, key_tile, ROWS, head, tiles)
                half_score = dot(k, q[head], ((1,), (1,))) * scale
                grad_probs = dot(v, grad[head], ((1,), (1,)))
                tanh = jnp.tanh(half_score)
                twice = 1.0 + tanh
                probs = jnp.where(allowed, half_score * twice, 0.0).astype(BF16)
                slope = twice * (1.0 + half_score * (1.0 - tanh))
                grad_scores = jnp.where(allowed, grad_probs * slope, 0.0).astype(BF16)
                slots = pl.ds(key_tile * 2, 2 * tiles)
                dk = dot(grad_scores, q[head], ((1,), (0,))).reshape(2 * tiles, ROWS, HEAD)
                dv = dot(probs, grad[head], ((1,), (0,))).reshape(2 * tiles, ROWS, HEAD)
                dkv_ref[slots, 0:ROWS, head_cols(head)] += dk
                dkv_ref[slots, ROWS : 2 * ROWS, head_cols(head)] += dv
                sums.append(total[head] + dot(k, grad_scores, ((0,), (0,))))
            return tuple(sums)

        total = tuple(dq_ref[head_cols(head), here] for head in range(2))
        total = over_keys(info, tile, back, step, total)
        for head in range(2):
            dq_ref[head_cols(head), here] = total[head]


def send_sums(dkv_ref, send_ref):
    scale = 0.5 / math.sqrt(HEAD)
    for slot in range(ZS):
        send_ref[slot, 0:ROWS, :] = (dkv_ref[slot, 0:ROWS, :] * scale).astype(BF16)
        send_ref[slot, ROWS : 2 * ROWS, :] = dkv_ref[slot, ROWS : 2 * ROWS, :].astype(BF16)


def backward_far_kernel(
    info, qd_ref, kv2_ref, att_ref, stats_ref, send_ref, grad_ref, dq_ref, gain_ref, dkv_ref
):
    make_grad_att(info, qd_ref, att_ref, stats_ref, grad_ref, gain_ref)
    dq_ref[...] = jnp.zeros_like(dq_ref)
    backward_tiles(info, 2, qd_ref, kv2_ref, grad_ref, dq_ref, dkv_ref)
    send_sums(dkv_ref, send_ref)


def backward_near_kernel(info, qd_ref, kv1_ref, grad_ref, dq_in_ref, send_ref, dq_ref, dkv_ref):
    dq_ref[...] = dq_in_ref[...]
    backward_tiles(info, 1, qd_ref, kv1_ref, grad_ref, dq_ref, dkv_ref)
    send_sums(dkv_ref, send_ref)


def backward_own_kernel(info, qd_ref, kv0_ref, grad_ref, dq_in_ref, dq_ref, dkv_ref):
    dq_ref[...] = dq_in_ref[...]
    backward_tiles(info, 0, qd_ref, kv0_ref, grad_ref, dq_ref, dkv_ref)


def join_kernel(dq_ref, dkv_ref, other1_ref, other2_ref, out_ref):
    scale = 0.5 / math.sqrt(HEAD)
    for slot in range(ZS):
        others = other1_ref[slot].astype(F32) + other2_ref[slot].astype(F32)
        dk = dkv_ref[slot, 0:ROWS, :] * scale + others[0:ROWS]
        dv = dkv_ref[slot, ROWS : 2 * ROWS, :] + others[ROWS : 2 * ROWS]
        out_ref[slot, 0:ROWS, :] = dk.astype(BF16)
        out_ref[slot, ROWS : 2 * ROWS, :] = dv.astype(BF16)
        for head in range(2):
            dq = dq_ref[head_cols(head), slot * ROWS : (slot + 1) * ROWS].T * scale
            out_ref[slot, 2 * ROWS : 3 * ROWS, head_cols(head)] = dq.astype(BF16)


def unpack_kernel(in_ref, gain_sum_ref, gain_ref, dq_ref, dk_ref, dv_ref, grad_gain_ref):
    grad_gain_ref[...] = gain_sum_ref[...] / gain_ref[...]
    for z in range(ZS):
        cols = slice(z * PAIR, (z + 1) * PAIR)
        dk_ref[:, cols] = in_ref[z, 0:ROWS, :]
        dv_ref[:, cols] = in_ref[z, ROWS : 2 * ROWS, :]
        dq_ref[:, cols] = in_ref[z, 2 * ROWS : 3 * ROWS, :]


def call(kernel, outs, *args, scalars=0, scratch=(), flops=1, space=pltpu.VMEM, limit=VMEM_LIMIT):
    specs = [pl.BlockSpec(memory_space=pltpu.SMEM)] * scalars
    specs += [pl.BlockSpec(memory_space=space)] * (len(args) - scalars)
    return pl.pallas_call(
        kernel,
        out_shape=outs,
        in_specs=specs,
        out_specs=[pl.BlockSpec(memory_space=space)] * len(outs),
        scratch_shapes=scratch,
        compiler_params=pltpu.CompilerParams(vmem_limit_bytes=limit),
        cost_estimate=pl.CostEstimate(flops=flops, bytes_accessed=0, transcendentals=0),
    )(*args)


def along_z(array):
    groups = [[y * ZS + z for z in range(ZS)] for y in range(ZS)]
    return lax.all_to_all(array, "seq", 0, 0, axis_index_groups=groups, tiled=True)


def shift_z(array, by):
    pairs = [(y * ZS + z, y * ZS + (z + by) % ZS) for y in range(ZS) for z in range(ZS)]
    return lax.ppermute(array, "seq", pairs)


def add_over(array, axis, low):
    size = lax.axis_size(axis)
    if 2 * low >= size:
        return array
    others = [
        lax.ppermute(array, axis, [(i, i ^ bits) for i in range(size)])
        for bits in (low, 2 * low, 3 * low)
    ]
    return (array + others[0]) + (others[1] + others[2])


def add_bits(array, axis, bits):
    size = lax.axis_size(axis)
    for bit in bits:
        if bit < size:
            array = array + lax.ppermute(array, axis, [(i, i ^ bit) for i in range(size)])
    return array


def add_pairs(array, axis):
    size = lax.axis_size(axis)
    if size == 1:
        return array
    return array + lax.ppermute(array, axis, [(i, i ^ 1) for i in range(size)])


def shift_y(array, by):
    devices = lax.axis_size("seq")
    pairs = [(i, i + ZS * by) for i in range(devices) if 0 <= i + ZS * by < devices]
    return lax.ppermute(array, "seq", pairs)


def per_device(queries, keys, values, gates, lengths, gain, grad_out):
    rows, width = queries.shape[1:]
    shape = jax.ShapeDtypeStruct
    ends = jnp.cumsum(lengths[0])
    info = jnp.concatenate([jnp.stack([lax.axis_index("seq")]), ends]).astype(jnp.int32)
    pair = shape((ZS, 2 * ROWS, PAIR), BF16)
    pair_sums = shape((ZS, 2 * ROWS, PAIR), F32)
    block = shape((BLOCK, PAIR), F32)
    turned = shape((PAIR, BLOCK), F32)
    sums_scratch = [pltpu.VMEM(pair_sums.shape, F32)]

    (kv,) = call(
        pack_kv_kernel,
        [pair],
        keys[0],
        values[0],
        space=pltpu.HBM,
        limit=62 * 1024 * 1024,
        scratch=[pltpu.SemaphoreType.DMA((2 * ZS,))],
    )
    kv0 = along_z(kv)
    kv2 = shift_y(kv0, 2)
    kv1 = shift_y(kv0, 1)
    (qd,) = call(pack_q_kernel, [pair], queries[0], gates[0], grad_out[0], gain[None])
    qd = along_z(qd)
    (own_sum,) = call(forward_own_kernel, [block], info, qd, kv0, scalars=1)
    attended, stats = call(
        forward_kernel,
        [block, shape((ZS, 4 * ZS, ROWS), F32)],
        info,
        qd,
        kv1,
        kv2,
        own_sum,
        scalars=1,
    )
    stats = along_z(stats)
    to2, grad_att, dq, gain_sum = call(
        backward_far_kernel,
        [pair, shape((ZS, ROWS, PAIR), BF16), turned, shape((2, HEAD), F32)],
        info,
        qd,
        kv2,
        attended,
        stats,
        scalars=1,
        scratch=sums_scratch,
    )
    from2 = shift_y(to2, -2)
    to1, dq = call(
        backward_near_kernel,
        [pair, turned],
        info,
        qd,
        kv1,
        grad_att,
        dq,
        scalars=1,
        scratch=sums_scratch,
    )
    from1 = shift_y(to1, -1)
    gain_sum, to1 = lax.optimization_barrier((gain_sum, to1))
    back = call(
        back_kernel,
        [shape((ROWS + EXTRA, PAIR), BF16)] * ZS,
        info,
        attended,
        gain_sum,
        scalars=1,
    )
    back = list(back)
    back[2] = shift_z(back[2], 2)
    back[1] = shift_z(back[1], 1)
    back[3] = shift_z(back[3], 3)
    dq, dkv = call(
        backward_own_kernel, [turned, pair_sums], info, qd, kv0, grad_att, dq, scalars=1
    )
    (gain_sum,) = call(gain_kernel, [shape((1, width), F32)], info, *back, scalars=1)
    output, grad_gate = call(
        norm_kernel,
        [shape((rows, width), BF16)] * 2,
        info,
        *back,
        gates[0],
        grad_out[0],
        gain[None],
        scalars=1,
    )
    (joined,) = call(join_kernel, [shape((ZS, 3 * ROWS, PAIR), BF16)], dq, dkv, from1, from2)
    gain_sum, joined = lax.optimization_barrier((gain_sum, joined))
    gain_sum = add_pairs(gain_sum, "own")
    gain_sum = add_bits(add_bits(add_bits(gain_sum, "own", (2, 4)), "seq", (4, 8)), "own", (8, 16))
    grad_q, grad_k, grad_v, grad_gain = call(
        unpack_kernel,
        [shape((rows, width), BF16)] * 3 + [shape((1, width), F32)],
        along_z(joined),
        gain_sum,
        gain[None],
    )
    return (output[None], grad_q[None], grad_k[None], grad_v[None], grad_gate[None], grad_gain[0])


def solution(mesh):
    wide = P("own", "seq", None)
    return jax.shard_map(
        per_device,
        mesh=mesh,
        in_specs=(wide, wide, wide, wide, P("own", None), P(), wide),
        out_specs=(wide, wide, wide, wide, wide, P()),
        check_vma=False,
    )
```
